32 devices in a mesh: dom: 8 (over z, x), grp: 4 (over y, core).
Axes of the slice: x: 2, y: 2, z: 4, core: 2. Of those that a mesh axis runs over, the one named last changes fastest.
Arguments:
- nodes: bfloat16 [32768, 256], P(('dom', 'grp')), may hold values from -6 to 6
- edges: bfloat16 [131072, 256], P(('dom', 'grp')), may hold values from -6 to 6
- senders: int32 [131072], P(('dom', 'grp')), may hold values from 0 to 1279, as said below
- receivers: int32 [131072], P(('dom', 'grp')), may hold values from 0 to 1023, as said below
- edge_count: int32 [32], P(('dom', 'grp')), may hold values from 64 to 512, as said below
- halo_rows: int32 [32, 8, 32], P(('dom', 'grp')), may hold values from 0 to 1023, as said below
- aggregates: int32 [32768], P(('dom', 'grp')), may hold values from 0 to 511, as said below
- coarse_edges: bfloat16 [8, 2048, 256], P('dom'), may hold values from -6 to 6
- coarse_senders: int32 [8, 2048], P('dom'), may hold values from 0 to 511
- coarse_receivers: int32 [8, 2048], P('dom'), may hold values from 0 to 127
- cotangent: bfloat16 [32768, 256], P(('dom', 'grp')), may hold values from -6 to 6
- fine_weights: bfloat16 [1792, 256], replicated, may hold values from -0.21875 to 0.21875
- coarse_weights: bfloat16 [1792, 256], replicated, may hold values from -0.21875 to 0.21875
Outputs:
- fine_out: bfloat16 [32768, 256], P(('dom', 'grp'))
- node_grad: bfloat16 [32768, 256], P(('dom', 'grp'))
- edge_grad: bfloat16 [131072, 256], P(('dom', 'grp'))
- fine_weight_grad: float32 [1792, 256], replicated
- coarse_weight_grad: float32 [1792, 256], replicated
The draws below stay inside these ranges and needn't reach their ends.
Inputs may be any that keep to these rules, and one draw needn't show every extreme that they name: `senders`: A value at least 1024 names a halo slot from a partition at another dom index with the same grp index. The receivers of edge slots 512 * t to 512 * t + 511 of a partition lie in its node rows 128 * t to 128 * t + 127. `edge_count`: each count is 512 divided by a power of two; some partition has 512 and some 64. `halo_rows`: entry [q, p, t] is a local node row of partition q; the rows of one list are distinct. `aggregates`: every coarse node of a group is the aggregate of exactly 8 fine nodes of that group.
All inputs are finite; a program needn't handle non-finite values.
Results may differ from the reference program's by a relative error of at most 0.035.
Values may be sent and summed in bfloat16 or wider, within the bound.
No kernel may reach another device: no remote copies, remote signals or barrier semaphores. Data moves between devices by JAX's collectives and lax.ppermute only.
A program may use at most 128 MiB of HBM per device.

```python
import jax
import jax.numpy as jnp
from jax import lax

LATENT = 256
NODE_DEV = 1024
SLOT = 32
NODES = 32768
EDGES = 131072
COARSE = 4096
COARSE_EDGES = 16384
N_DOM = 8
N_GRP = 4


def pair_counts(key):
    seeded = jax.random.fold_in(key, 101)
    counts = jax.random.randint(jax.random.fold_in(seeded, 1), (N_DOM, N_GRP, N_DOM), 1, SLOT + 1)
    domain = jnp.arange(N_DOM, dtype=jnp.int32)
    chosen = (domain[:, None] + 1 + jax.random.randint(jax.random.fold_in(seeded, 2), (N_DOM, N_GRP), 0, N_DOM - 1)) % N_DOM
    counts = jnp.where(domain[None, None, :] == chosen[:, :, None], SLOT, counts)
    counts = jnp.where(domain[None, None, :] == domain[:, None, None], 0, counts)
    return counts.at[N_DOM - 1, 0, 0].set(SLOT)


def draw_senders(key, part):
    counts = pair_counts(key)
    key = jax.random.fold_in(key, 3)
    edge_ids = jnp.arange(EDGES, dtype=jnp.int32)
    holder = edge_ids // (4 * NODE_DEV)
    home_dom = holder // N_GRP
    home_group = holder % N_GRP
    remote = jax.random.randint(jax.random.fold_in(key, 1), (EDGES,), 0, 3) == 0
    nearby = jax.random.randint(jax.random.fold_in(key, 2), (EDGES,), 0, NODE_DEV)
    partner = (home_dom + 1 + jax.random.randint(jax.random.fold_in(key, 4), (EDGES,), 0, N_DOM - 1)) % N_DOM
    filled = counts[partner, home_group, home_dom]
    slot_pick = jax.random.randint(jax.random.fold_in(key, 5), (EDGES,), 0, filled)
    picked = jnp.where(remote, NODE_DEV + partner * SLOT + slot_pick, nearby).astype(jnp.int32)
    return picked.at[0].set(NODE_DEV + N_DOM * SLOT - 1).at[1].set(0).astype(jnp.int32)


def draw_receivers(key, part):
    key = jax.random.fold_in(key, 7)
    edge_ids = jnp.arange(EDGES, dtype=jnp.int32)
    tile_index = edge_ids % (4 * NODE_DEV) // 512
    return (tile_index * 128 + jax.random.randint(key, (EDGES,), 0, 128)).astype(jnp.int32)


def draw_edge_count(key, part):
    key = jax.random.fold_in(key, 9)
    devices = N_DOM * N_GRP
    halving = jax.random.randint(jax.random.fold_in(key, 1), (devices,), 0, 4)
    busiest = jax.random.randint(jax.random.fold_in(key, 2), (), 0, devices)
    lightest = (busiest + 1 + jax.random.randint(jax.random.fold_in(key, 3), (), 0, devices - 1)) % devices
    device_ids = jnp.arange(devices, dtype=jnp.int32)
    halving = jnp.where(device_ids == busiest, 0, jnp.where(device_ids == lightest, 3, halving))
    return jnp.right_shift(jnp.full((devices,), 512, jnp.int32), halving).astype(jnp.int32)


def draw_halo_rows(key, part):
    key = jax.random.fold_in(key, 13)
    devices = N_DOM * N_GRP
    scores = jax.random.randint(key, (devices, N_DOM, NODE_DEV), 0, 2 ** 20) * NODE_DEV + jnp.arange(NODE_DEV, dtype=jnp.int32)
    scores = scores.at[0, 0, NODE_DEV - 1].set(-2).at[0, 0, 0].set(-1)
    ranked = jnp.argsort(scores, axis=-1)
    return ranked[:, :, :SLOT].astype(jnp.int32)


def draw_aggregates(key, part):
    key = jax.random.fold_in(key, 17)
    subkeys = jax.random.split(key, N_DOM)

    def shuffle_group(subkey):
        return jax.random.permutation(subkey, N_GRP * NODE_DEV)
    shuffles = jax.vmap(shuffle_group)(subkeys)
    return (shuffles // 8).reshape(-1).astype(jnp.int32)


def draw_coarse_senders(key, part):
    key = jax.random.fold_in(key, 19)
    picked = jax.random.randint(key, (N_DOM, N_GRP * NODE_DEV // 2), 0, N_GRP * (NODE_DEV // 8)).astype(jnp.int32)
    return picked.at[0, 0].set(0).at[0, 1].set(N_GRP * (NODE_DEV // 8) - 1).astype(jnp.int32)


def draw_coarse_receivers(key, part):
    key = jax.random.fold_in(key, 23)
    picked = jax.random.randint(key, (N_DOM, N_GRP * NODE_DEV // 2), 0, NODE_DEV // 8).astype(jnp.int32)
    return picked.at[0, 0].set(0).at[0, 1].set(NODE_DEV // 8 - 1).astype(jnp.int32)


def shard_levels(rng, dims, cuts, low, largest):
    def one(dim, shards_of):
        heights = jax.random.uniform(jax.random.fold_in(jax.random.fold_in(rng, 6), dim), (shards_of,), jnp.float32, low / len(cuts), largest / len(cuts))
        return jnp.repeat(jnp.exp(heights), dims[dim] // shards_of).reshape((-1,) + (1,) * (len(dims) - dim - 1))

    level = one(*cuts[0])
    for cut in cuts[1:]:
        level = level * one(*cut)
    return level


def noise(own_key, extent, scale, limit, shards=(), kind=jnp.bfloat16):
    values = scale * jax.random.normal(own_key, extent, jnp.float32)
    if shards:
        values = values * shard_levels(own_key, extent, shards, -0.22, 0.18)
    return jnp.clip(values, -limit, limit).astype(kind)


def setup_inputs(seed: int = 0) -> dict:
    key_of = jax.random.split(jax.random.key(seed), 14)
    return {
        "nodes": noise(key_of[0], (NODES, LATENT), 1.0, 6.0, ((0, 32),)),
        "edges": noise(key_of[1], (EDGES, LATENT), 1.0, 6.0, ((0, 32),)),
        "senders": draw_senders(jax.random.fold_in(key_of[13], 71), 0),
        "receivers": draw_receivers(jax.random.fold_in(key_of[13], 71), 0),
        "edge_count": draw_edge_count(jax.random.fold_in(key_of[13], 71), 0),
        "halo_rows": draw_halo_rows(jax.random.fold_in(key_of[13], 71), 0),
        "aggregates": draw_aggregates(jax.random.fold_in(key_of[13], 71), 0),
        "coarse_edges": noise(key_of[7], (N_DOM, N_GRP * NODE_DEV // 2, LATENT), 1.0, 6.0, ((0, 8),)),
        "coarse_senders": draw_coarse_senders(jax.random.fold_in(key_of[13], 71), 0),
        "coarse_receivers": draw_coarse_receivers(jax.random.fold_in(key_of[13], 71), 0),
        "cotangent": noise(key_of[10], (NODES, LATENT), 1.0, 6.0, ((0, 32),)),
        "fine_weights": noise(key_of[11], (7 * LATENT, LATENT), (3 * LATENT) ** -0.5, 0.21875),
        "coarse_weights": noise(key_of[12], (7 * LATENT, LATENT), (3 * LATENT) ** -0.5, 0.21875),
    }


def stored(values):
    return lax.optimization_barrier(values.astype(jnp.bfloat16))

def layer_norm(values):
    centre = values - lax.optimization_barrier(jnp.mean(values, axis=-1, keepdims=True))
    spread = lax.optimization_barrier(jnp.mean(centre * centre, axis=-1, keepdims=True))
    return centre * lax.rsqrt(spread + 1e-05)

def two_layer(inputs, first, second):
    hidden = jnp.dot(inputs, first, preferred_element_type=jnp.float32)
    active = jax.nn.silu(hidden).astype(jnp.bfloat16)
    return layer_norm(jnp.dot(active, second, preferred_element_type=jnp.float32))

def edge_message(edge_rows, sender_rows, target_rows, weights):
    feat_width = edge_rows.shape[1]
    narrow = weights.astype(jnp.bfloat16)
    joined = jnp.concatenate([edge_rows, sender_rows, target_rows], axis=1)
    return stored(two_layer(joined, narrow[:3 * feat_width], narrow[3 * feat_width:4 * feat_width]))

def node_update(node_rows, summed, weights):
    feat_width = node_rows.shape[1]
    narrow = weights.astype(jnp.bfloat16)
    joined = jnp.concatenate([node_rows, summed], axis=1)
    change = two_layer(joined, narrow[4 * feat_width:6 * feat_width], narrow[6 * feat_width:])
    return stored(node_rows.astype(jnp.float32) + change)

def reference(nodes, edges, senders, receivers, edge_count, halo_rows, aggregates, coarse_edges, coarse_senders, coarse_receivers, cotangent, fine_weights, coarse_weights):
    devices = N_DOM * N_GRP
    per_dev = 4 * NODE_DEV
    own_rows = NODE_DEV // 8
    group_rows = own_rows * N_GRP
    per_block = coarse_senders.shape[1] // N_GRP
    edge_ids = jnp.arange(EDGES, dtype=jnp.int32)
    holder = edge_ids // per_dev
    home_dom = holder // N_GRP
    home_group = holder % N_GRP
    offset = jnp.maximum(senders - NODE_DEV, 0)
    source = offset // SLOT * N_GRP + home_group
    far_row = halo_rows[source, home_dom, offset % SLOT]
    global_send = jnp.where(senders < NODE_DEV, holder * NODE_DEV + senders, source * NODE_DEV + far_row).astype(jnp.int32)
    global_recv = (holder * NODE_DEV + receivers).astype(jnp.int32)
    live_mask = edge_ids % per_dev % 512 < edge_count[holder]
    node_ids = jnp.arange(NODES, dtype=jnp.int32)
    coarse_of = (node_ids // (N_GRP * NODE_DEV) * group_rows + aggregates).astype(jnp.int32)
    coarse_ids = jnp.arange(COARSE_EDGES, dtype=jnp.int32)
    coarse_group = coarse_ids // (N_GRP * per_block)
    coarse_send = (coarse_group * group_rows + coarse_senders.reshape(-1)).astype(jnp.int32)
    coarse_recv = (coarse_group * group_rows + coarse_ids // per_block % N_GRP * own_rows + coarse_receivers.reshape(-1)).astype(jnp.int32)
    flat_coarse = coarse_edges.reshape(COARSE_EDGES, LATENT)

    def forward(node_values, edge_values, fine_float, coarse_float):
        node_wide = node_values.astype(jnp.float32)

        def edge_block(pieces):
            edge_rows, send_rows, recv_rows, recv_local, live_rows = pieces
            messages = edge_message(edge_rows, jnp.take(node_wide, send_rows, axis=0).astype(jnp.bfloat16), jnp.take(node_wide, recv_rows, axis=0).astype(jnp.bfloat16), fine_float)
            kept = jnp.where(live_rows[:, None], messages.astype(jnp.float32), 0.0)
            return jax.ops.segment_sum(kept, recv_local, num_segments=NODE_DEV).astype(jnp.bfloat16)
        summed = lax.map(jax.checkpoint(edge_block), (edge_values.reshape(devices, per_dev, LATENT), global_send.reshape(devices, per_dev), global_recv.reshape(devices, per_dev), receivers.reshape(devices, per_dev), live_mask.reshape(devices, per_dev)))
        refined = node_update(node_wide.astype(jnp.bfloat16), summed.reshape(NODES, LATENT), fine_float)
        refined_wide = refined.astype(jnp.float32)
        coarse_input = stored(jax.ops.segment_sum(refined_wide, coarse_of, num_segments=COARSE) * 0.125)
        coarse_wide = coarse_input.astype(jnp.float32)
        coarse_messages = edge_message(flat_coarse, jnp.take(coarse_wide, coarse_send, axis=0).astype(jnp.bfloat16), jnp.take(coarse_wide, coarse_recv, axis=0).astype(jnp.bfloat16), coarse_float)
        coarse_summed = jax.ops.segment_sum(coarse_messages.astype(jnp.float32), coarse_recv, num_segments=COARSE).astype(jnp.bfloat16)
        coarse_output = node_update(coarse_wide.astype(jnp.bfloat16), coarse_summed, coarse_float)
        lifted = jnp.take(coarse_output.astype(jnp.float32), coarse_of, axis=0)
        return (refined_wide + lifted).astype(jnp.bfloat16)
    fine_out, backward = jax.vjp(forward, nodes, edges, fine_weights.astype(jnp.float32), coarse_weights.astype(jnp.float32))
    node_grad, edge_grad, fine_grad, coarse_grad = backward(cotangent)
    return (fine_out, node_grad, edge_grad, fine_grad * EDGES ** (-0.5), coarse_grad * COARSE_EDGES ** (-0.5))
```

```python
import functools

import jax
import jax.numpy as jnp
from jax import lax
from jax.experimental import pallas as pl
from jax.experimental.pallas import tpu as pltpu
from jax.sharding import PartitionSpec as P

F32 = jnp.float32
BF16 = jnp.bfloat16
ROWS = 128
MIB = 1024 * 1024
CHUNK = 32
I16 = jnp.int16


def mm(a, b):
    return lax.dot_general(a, b, (((1,), (0,)), ((), ())), preferred_element_type=F32)


def mm_nt(a, b):
    return lax.dot_general(a, b, (((1,), (1,)), ((), ())), preferred_element_type=F32)


def mm_tn(a, b):
    return lax.dot_general(a, b, (((0,), (0,)), ((), ())), preferred_element_type=F32)


def column(row):
    return jnp.broadcast_to(row, (128, row.shape[1])).T.astype(I16)


def flags(mask):
    return jnp.where(mask, jnp.ones((), BF16), jnp.zeros((), BF16))


def pick_rows(rows, width):
    lane = lax.broadcasted_iota(jnp.int32, (rows[0].shape[1], 128), 1).astype(I16)
    out = []
    for row in rows:
        index = column(row)
        out.append(
            jnp.concatenate([flags(index == lane + I16(128 * k)) for k in range(width // 128)], axis=1)
        )
    return out[0] if len(out) == 1 else jnp.concatenate(out, axis=0)


def pick_columns(rows, height):
    sub = lax.broadcasted_iota(jnp.int32, (height, rows[0].shape[1]), 0).astype(I16)
    out = []
    for row in rows:
        index = jnp.broadcast_to(row, (16, row.shape[1])).astype(I16)
        out.append(flags(sub == jnp.broadcast_to(index[0:1, :], sub.shape)))
    return out[0] if len(out) == 1 else jnp.concatenate(out, axis=1)


def gate(hidden):
    return 0.5 + 0.5 * jnp.tanh(0.5 * hidden)


def normalise(values):
    centre = values - jnp.mean(values, axis=-1, keepdims=True)
    spread = jnp.mean(centre * centre, axis=-1, keepdims=True)
    scale = lax.rsqrt(spread + 1e-05)
    return centre * scale, scale


def normalise_back(grad, unit, scale):
    along = jnp.mean(grad * unit, axis=-1, keepdims=True)
    return scale * (grad - jnp.mean(grad, axis=-1, keepdims=True) - unit * along)


def kernel_call(kernel, micros, limit, **kwargs):
    return pl.pallas_call(
        kernel,
        compiler_params=pltpu.CompilerParams(vmem_limit_bytes=limit * MIB),
        cost_estimate=pl.CostEstimate(
            flops=int(micros * 1.1e9), bytes_accessed=1 << 20, transcendentals=0
        ),
        **kwargs,
    )


def smem():
    return pl.BlockSpec(memory_space=pltpu.SMEM)


def whole(array):
    return pl.BlockSpec(array.shape, lambda t: (0,) * len(array.shape))


def by_tile(rows, columns):
    return pl.BlockSpec((rows, columns), lambda t: (t, 0))


def shape(rows, columns, dtype=BF16):
    return jax.ShapeDtypeStruct((rows, columns), dtype)


def index_rows(ref, start, count):
    return [ref[pl.ds(start + j, 1), :] for j in range(count)]


def live_rows(step, receivers, count, tile, spans):
    lane = lax.broadcasted_iota(jnp.int32, (1, 128), 1)
    parts = tile // 128
    out = []
    for s in range(spans):
        block = step * spans + s
        rows = index_rows(receivers, block * parts, parts)
        out.append(
            [
                jnp.where(lane + 128 * j < count[0], row - block * ROWS, -1)
                for j, row in enumerate(rows)
            ]
        )
    return out


def chunks(total):
    return [slice(r, r + CHUNK) for r in range(0, total, CHUNK)]


def moved(start, here):
    return pl.ds(pl.multiple_of(start + here.start, CHUNK), here.stop - here.start)


def fill_rows(ref, rows, width):
    for j, row in enumerate(rows):
        ref[j * 128 : (j + 1) * 128, :] = pick_rows([row], width)


def my_core():
    return lax.rem(lax.axis_index("grp"), 2)


def split_halves(ref, mine_out, other_out):
    half = mine_out.shape[0]
    core = my_core()
    mine_out[...] = ref[pl.ds(core * half, half), :]
    other_out[...] = ref[pl.ds((1 - core) * half, half), :]


def send_kernel(nodes, halo, near_out, far_out):
    doms, slots = halo.shape
    me = lax.axis_index("dom")
    for first, out in ((0, near_out), (doms // 2, far_out)):
        picks = [
            pick_rows([halo[pl.ds(jnp.bitwise_xor(me, first + r), 1), :]], nodes.shape[0])
            for r in range(doms // 2)
        ]
        out[...] = mm(jnp.concatenate(picks, axis=0), nodes[...]).astype(BF16)


def gather_slots(places, refs, out):
    slots = out.shape[0] // len(places)
    for r, (which, slot) in enumerate(places):
        out[r * slots : (r + 1) * slots, :] = refs[which][slot * slots : (slot + 1) * slots, :]


def group_sums(aggregates, values, mine_out, other_out, sums):
    rows = [aggregates[k : k + 1, :] for k in range(aggregates.shape[0])]
    sums[...] = mm(pick_columns(rows, sums.shape[0]), values).astype(BF16)
    split_halves(sums, mine_out, other_out)


def cotangent_kernel(aggregates, cotangent, mine_out, other_out, sums):
    group_sums(aggregates, cotangent[...], mine_out, other_out, sums)


def fine_local_kernel(
    tile, step_edges, count, edges, senders, receivers, nodes, weights,
    partial_out, send_proj, recv_proj, pick,
):
    width = nodes.shape[1]
    spans = step_edges // tile
    send_proj[...] = mm(nodes[...], weights[width : 2 * width, :]).astype(BF16)
    recv_proj[...] = mm(nodes[...], weights[2 * width : 3 * width, :]).astype(BF16)

    def run(step, carry):
        start = step * step_edges
        send_rows = index_rows(senders, step * spans * (tile // 128), spans * (tile // 128))
        recv_rows = live_rows(step, receivers, count, tile, spans)
        fill_rows(pick, send_rows, nodes.shape[0])
        for s in range(spans):
            own = pl.ds((step * spans + s) * ROWS, ROWS)
            here = slice(s * tile, (s + 1) * tile)
            there = moved(start, here)
            partial_out[there, :] = (
                mm(edges[there, :], weights[:width, :])
                + mm(pick_rows(recv_rows[s], ROWS), recv_proj[own, :])
                + mm(pick[here, :], send_proj[...])
            ).astype(BF16)
        return carry

    lax.fori_loop(0, edges.shape[0] // step_edges, run, 0)


def activate(hidden, active_out, slope_out, here):
    opened = gate(hidden)
    active = hidden * opened
    active_out[here, :] = active.astype(BF16)
    slope_out[here, :] = (opened + active * (1.0 - opened)).astype(BF16)


def fine_halo_kernel(
    tile, places, count, partial, senders, receivers, aggregates, nodes, weights, *refs
):
    pieces = refs[: -(13 + 5)]
    (
    active_out, slope_out, unit_out, scale_out,
    node_active_out, node_slope_out, node_unit_out, node_scale_out, summed_out, refined_out,
    mine_out, other_out, halo,
    halo_proj, pick, wide, wide_next, sums,
    ) = refs[-(13 + 5) :]
    step = pl.program_id(0)
    node_count, width = nodes.shape
    spans = partial.shape[0] // tile

    @pl.when(step == 0)
    def _():
        gather_slots(places, pieces, halo)
        halo_proj[...] = mm(halo[...], weights[width : 2 * width, :]).astype(BF16)

    send_rows = index_rows(senders, step * spans * (tile // 128), spans * (tile // 128))
    recv_rows = live_rows(step, receivers, count, tile, spans)
    mask = lax.axis_index("dom") * (halo.shape[0] // len(places))
    fill_rows(
        pick, [jnp.bitwise_xor(row - node_count, mask) for row in send_rows], halo.shape[0]
    )
    wide[...] = mm(pick[...], halo_proj[...])
    for here in chunks(partial.shape[0]):
        activate(partial[here, :].astype(F32) + wide[here, :], active_out, slope_out, here)
    wide_next[...] = mm(active_out[...], weights[3 * width : 4 * width, :])
    for here in chunks(partial.shape[0]):
        unit, scale = normalise(wide_next[here, :])
        unit_out[here, :] = unit.astype(BF16)
        scale_out[here, :] = scale
    for s in range(spans):
        own = pl.ds((step * spans + s) * ROWS, ROWS)
        summed_out[own, :] = mm(
            pick_columns(recv_rows[s], ROWS), unit_out[s * tile : (s + 1) * tile, :]
        ).astype(BF16)

    @pl.when(step == pl.num_programs(0) - 1)
    def _():
        wide[:node_count, :] = mm(nodes[...], weights[4 * width : 5 * width, :]) + mm(
            summed_out[...], weights[5 * width : 6 * width, :]
        )
        for here in chunks(node_count):
            activate(wide[here, :], node_active_out, node_slope_out, here)
        wide_next[:node_count, :] = mm(node_active_out[...], weights[6 * width :, :])
        for here in chunks(node_count):
            unit, scale = normalise(wide_next[here, :])
            node_unit_out[here, :] = unit.astype(BF16)
            node_scale_out[here, :] = scale
            refined_out[here, :] = (nodes[here, :].astype(F32) + unit).astype(BF16)
        group_sums(aggregates, refined_out[...], mine_out, other_out, sums)


def coarse_kernel(
    groups, chunk,
    table_mine, table_other, cot_mine, cot_other, edges, senders, receivers, weights,
    output_out, grad_out, weight_mine, weight_other,
    table, cot, send_proj, recv_proj, recv_sum, summed, summed_grad,
    node_active, node_slope, node_unit, node_pre, node_hidden_grad,
    active_all, slope_all, unit_all, scale_all, hidden_grad_all, pre_all,
    pick, wide, wide_next, node_scale, own_grad, weight_all,
):
    group_rows, width = table.shape
    half = group_rows // 2
    total = edges.shape[0]
    tile = total // groups
    spans = chunk // tile
    parts = chunk // 128
    steps = total // chunk
    core = my_core()
    mine = pl.ds(core * half, half)
    other = pl.ds((1 - core) * half, half)
    table[mine, :] = table_mine[...]
    table[other, :] = table_other[...]
    cot[mine, :] = cot_mine[...]
    cot[other, :] = cot_other[...]
    send_proj[...] = mm(table[...], weights[width : 2 * width, :]).astype(BF16)
    recv_proj[...] = mm(table[...], weights[2 * width : 3 * width, :]).astype(BF16)

    def recv_at(i, s):
        return index_rows(receivers, i * parts + s * (tile // 128), tile // 128)

    def forward(i, carry):
        start = pl.multiple_of(i * chunk, chunk)
        all_here = pl.ds(start, chunk)
        fill_rows(pick, index_rows(senders, i * parts, parts), group_rows)
        for s in range(spans):
            own = pl.ds((i * spans + s) * ROWS, ROWS)
            here = slice(s * tile, (s + 1) * tile)
            wide[here, :] = (
                mm(edges[pl.ds(start + s * tile, tile), :], weights[:width, :])
                + mm(pick_rows(recv_at(i, s), ROWS), recv_proj[own, :])
                + mm(pick[here, :], send_proj[...])
            )
        for here in chunks(chunk):
            activate(wide[here, :], active_all, slope_all, pl.ds(start + here.start, CHUNK))
        wide_next[...] = mm(active_all[all_here, :], weights[3 * width : 4 * width, :])
        for here in chunks(chunk):
            unit, scale = normalise(wide_next[here, :])
            unit_all[pl.ds(start + here.start, CHUNK), :] = unit.astype(BF16)
            scale_all[pl.ds(start + here.start, CHUNK), :] = scale
        for s in range(spans):
            own = pl.ds((i * spans + s) * ROWS, ROWS)
            summed[own, :] = mm(
                pick_columns(recv_at(i, s), ROWS), unit_all[pl.ds(start + s * tile, tile), :]
            ).astype(BF16)
        return carry

    lax.fori_loop(0, steps, forward, 0)

    nodes_here = slice(0, group_rows)
    wide[nodes_here, :] = mm(table[...], weights[4 * width : 5 * width, :]) + mm(
        summed[...], weights[5 * width : 6 * width, :]
    )
    for here in chunks(group_rows):
        activate(wide[here, :], node_active, node_slope, here)
    wide_next[nodes_here, :] = mm(node_active[...], weights[6 * width :, :])
    for here in chunks(group_rows):
        unit, scale = normalise(wide_next[here, :])
        output_out[here, :] = (table[here, :].astype(F32) + unit).astype(BF16)
        node_pre[here, :] = normalise_back(cot[here, :].astype(F32), unit, scale).astype(BF16)
    wide[nodes_here, :] = mm_nt(node_pre[...], weights[6 * width :, :])
    for here in chunks(group_rows):
        node_hidden_grad[here, :] = (wide[here, :] * node_slope[here, :].astype(F32)).astype(BF16)
    summed_grad[...] = mm_nt(
        node_hidden_grad[...], weights[5 * width : 6 * width, :]
    ).astype(BF16)
    own_grad[...] = mm_nt(node_hidden_grad[...], weights[4 * width : 5 * width, :])

    def backward(i, send_sum):
        start = pl.multiple_of(i * chunk, chunk)
        all_here = pl.ds(start, chunk)
        for s in range(spans):
            own = pl.ds((i * spans + s) * ROWS, ROWS)
            wide[s * tile : (s + 1) * tile, :] = mm(
                pick_rows(recv_at(i, s), ROWS), summed_grad[own, :]
            )
        for here in chunks(chunk):
            there = pl.ds(start + here.start, CHUNK)
            pre_all[there, :] = normalise_back(
                wide[here, :], unit_all[there, :].astype(F32), scale_all[there, :]
            ).astype(BF16)
        wide_next[...] = mm_nt(pre_all[all_here, :], weights[3 * width : 4 * width, :])
        for here in chunks(chunk):
            there = pl.ds(start + here.start, CHUNK)
            hidden_grad_all[there, :] = (
                wide_next[here, :] * slope_all[there, :].astype(F32)
            ).astype(BF16)
        for s in range(spans):
            own = pl.ds((i * spans + s) * ROWS, ROWS)
            recv_sum[own, :] = mm(
                pick_columns(recv_at(i, s), ROWS),
                hidden_grad_all[pl.ds(start + s * tile, tile), :],
            ).astype(BF16)
        return send_sum + mm(
            pick_columns(index_rows(senders, i * parts, parts), group_rows),
            hidden_grad_all[all_here, :],
        )

    send_total = lax.fori_loop(
        0, steps, backward, jnp.zeros((group_rows, width), F32)
    ).astype(BF16)
    recv_total = recv_sum[...]
    grad_out[...] = (
        cot[...].astype(F32)
        + own_grad[...]
        + mm_nt(send_total, weights[width : 2 * width, :])
        + mm_nt(recv_total, weights[2 * width : 3 * width, :])
    ).astype(BF16)
    share = weight_mine.shape[0] * 2
    begin = (core * (groups // 2) + lax.axis_index("grp") // 2) * share
    products = [
        lambda: mm_tn(edges[...], hidden_grad_all[...]),
        lambda: mm_tn(table[...], send_total),
        lambda: mm_tn(table[...], recv_total),
        lambda: mm_tn(active_all[...], pre_all[...]),
        lambda: mm_tn(table[...], node_hidden_grad[...]),
        lambda: mm_tn(summed[...], node_hidden_grad[...]),
        lambda: mm_tn(node_active[...], node_pre[...]),
    ]
    for b, product in enumerate(products):

        @pl.when((b * width < begin + share) & ((b + 1) * width > begin))
        def _():
            weight_all[b * width : (b + 1) * width, :] = product()

    chunk_rows = share // 4
    place = coarse_place()
    for r in range(4):
        first = pl.multiple_of(begin + jnp.bitwise_xor(place, r) * chunk_rows, 8)
        out = (weight_mine, weight_other)[r // 2]
        here = slice((r % 2) * chunk_rows, (r % 2 + 1) * chunk_rows)
        out[here, :] = weight_all[pl.ds(first, chunk_rows), :].astype(BF16)


def coarse_place():
    dom = lax.axis_index("dom")
    return lax.rem(dom, 2) * 2 + lax.rem(dom // 2, 2)


def relative_chunks(ref, place, mine, other):
    rows = ref.shape[0] // 16
    for r in range(16):
        first = pl.multiple_of(jnp.bitwise_xor(place, r) * rows, 16)
        out = (mine, other)[r // 8]
        out[(r % 8) * rows : (r % 8 + 1) * rows, :] = ref[pl.ds(first, rows), :]


def fine_place():
    grp = lax.axis_index("grp")
    return lax.rem(grp, 2) * 8 + lax.rem(grp // 2, 2) * 4 + coarse_place()


def node_back_kernel(
    aggregates, table_grad, cotangent, node_active, node_slope, node_unit, node_scale, summed,
    nodes, weights,
    node_grad_out, summed_grad_out, weight_mine, weight_other,
    pre, hidden_grad, wide, wide_next, weight_out,
):
    node_count, width = nodes.shape
    rows = [aggregates[k : k + 1, :] for k in range(aggregates.shape[0])]
    wide[...] = mm(pick_rows(rows, table_grad.shape[0]), table_grad[...])
    for here in chunks(node_count):
        grad = (cotangent[here, :].astype(F32) + 0.125 * wide[here, :]).astype(BF16)
        grad = grad.astype(F32)
        node_grad_out[here, :] = grad
        pre[here, :] = normalise_back(
            grad, node_unit[here, :].astype(F32), node_scale[here, :]
        ).astype(BF16)
    wide_next[...] = mm_nt(pre[...], weights[6 * width :, :])
    for here in chunks(node_count):
        hidden_grad[here, :] = (
            wide_next[here, :] * node_slope[here, :].astype(F32)
        ).astype(BF16)
    summed_grad_out[...] = mm_nt(
        hidden_grad[...], weights[5 * width : 6 * width, :]
    ).astype(BF16)
    node_grad_out[...] += mm_nt(hidden_grad[...], weights[4 * width : 5 * width, :])
    weight_out[:width, :] = mm_tn(nodes[...], hidden_grad[...]).astype(BF16)
    weight_out[width : 2 * width, :] = mm_tn(summed[...], hidden_grad[...]).astype(BF16)
    weight_out[2 * width :, :] = mm_tn(node_active[...], pre[...]).astype(BF16)
    relative_chunks(weight_out, fine_place(), weight_mine, weight_other)


def edge_back(
    tile, slots, first_step, step_edges, count, edges, active, slope, unit, scale, senders,
    receivers, summed_grad, weights, hidden_grad_out, recv_sum, send_sum, first_grad, second_grad,
    pre, wide, wide_next,
):
    width = weights.shape[1]
    spans = step_edges // tile
    node_count = summed_grad.shape[0]
    mask = lax.axis_index("dom") * slots

    def run(i, carry):
        step = first_step + i
        start = step * step_edges
        begin = i * step_edges
        all_here = moved(start, slice(0, step_edges))
        all_out = moved(begin, slice(0, step_edges))
        send_rows = [
            jnp.where(row < node_count, row, jnp.bitwise_xor(row - node_count, mask) + node_count)
            for row in index_rows(senders, step * spans * (tile // 128), spans * (tile // 128))
        ]
        recv_rows = live_rows(step, receivers, count, tile, spans)
        for s in range(spans):
            own = pl.ds((step * spans + s) * ROWS, ROWS)
            wide[s * tile : (s + 1) * tile, :] = mm(
                pick_rows(recv_rows[s], ROWS), summed_grad[own, :]
            )
        for here in chunks(step_edges):
            there = moved(start, here)
            pre[here, :] = normalise_back(
                wide[here, :], unit[there, :].astype(F32), scale[there, :]
            ).astype(BF16)
        wide_next[...] = mm_nt(pre[...], weights[3 * width : 4 * width, :])
        for here in chunks(step_edges):
            hidden_grad_out[moved(begin, here), :] = (
                wide_next[here, :] * slope[moved(start, here), :].astype(F32)
            ).astype(BF16)
        hidden_grad = hidden_grad_out[all_out, :]
        second_grad[...] += mm_tn(active[all_here, :], pre[...])
        first_grad[...] += mm_tn(edges[all_here, :], hidden_grad)
        send_sum[...] += mm(pick_columns(send_rows, send_sum.shape[0]), hidden_grad)
        for s in range(spans):
            recv_sum[pl.ds((i * spans + s) * ROWS, ROWS), :] = mm(
                pick_columns(recv_rows[s], ROWS),
                hidden_grad_out[moved(begin, slice(s * tile, (s + 1) * tile)), :],
            ).astype(BF16)
        return carry

    lax.fori_loop(0, hidden_grad_out.shape[0] // step_edges, run, 0)


def edge_back_kernel(part, last, tile, slots, step_edges, *refs):
    (
        count, edges, active, slope, unit, scale, senders, receivers, summed_grad, weights,
    ) = refs[:10]
    refs = refs[10:]
    before = ()
    if part:
        before, refs = refs[:3], refs[3:]
    if last:
        nodes, halo, *recv_before = refs[: 2 + part]
        (
            hidden_grad_out, near_out, recv_out, weight_mine, weight_other, halo_near, halo_far,
            recv_sum, send_sum, first_grad, second_grad, pre, wide, wide_next, weight_all,
        ) = refs[2 + part :]
    else:
        (
            hidden_grad_out, recv_sum, send_sum, first_grad, second_grad, pre, wide, wide_next,
        ) = refs
    for i, total in enumerate((send_sum, first_grad, second_grad)):
        total[...] = before[i][...] if part else jnp.zeros_like(total)
    edge_back(
        tile, slots, part, step_edges, count, edges, active, slope, unit, scale, senders,
        receivers, summed_grad, weights, hidden_grad_out, recv_sum, send_sum, first_grad,
        second_grad, pre, wide, wide_next,
    )
    if not last:
        return
    node_count, width = nodes.shape
    send_total = send_sum[...].astype(BF16)
    near, far = send_total[:node_count, :], send_total[node_count:, :]
    for i, rows in enumerate([*recv_before, recv_sum]):
        recv_out[i * rows.shape[0] : (i + 1) * rows.shape[0], :] = rows[...]
    near_out[...] = near
    far_half = far.shape[0] // 2
    send_weights = weights[width : 2 * width, :]
    halo_near[...] = mm_nt(far[:far_half, :], send_weights).astype(BF16)
    halo_far[...] = mm_nt(far[far_half:, :], send_weights).astype(BF16)
    weight_all[:width, :] = first_grad[...].astype(BF16)
    weight_all[width : 2 * width, :] = (mm_tn(nodes[...], near) + mm_tn(halo[...], far)).astype(
        BF16
    )
    weight_all[2 * width : 3 * width, :] = mm_tn(nodes[...], recv_out[...]).astype(BF16)
    weight_all[3 * width : 4 * width, :] = second_grad[...].astype(BF16)
    relative_chunks(weight_all, fine_place(), weight_mine, weight_other)


def edge_out_kernel(weights, *refs):
    step = pl.program_id(0)
    width = weights.shape[1]
    for i, hidden_grad in enumerate(refs[:-1]):

        @pl.when(step == i)
        def _():
            refs[-1][...] = mm_nt(hidden_grad[...], weights[:width, :]).astype(BF16)


def fine_out_kernel(aggregates, table, refined, fine_out):
    rows = [aggregates[k : k + 1, :] for k in range(aggregates.shape[0])]
    lifted = mm(pick_rows(rows, table.shape[0]), table[...])
    fine_out[...] = (refined[...].astype(F32) + lifted).astype(BF16)


def return_kernel(places, halo, node_grad, near, recv_total, weights, *refs):
    doms = len(places)
    pieces, out, values = refs[:-2], refs[-2], refs[-1]
    width = out.shape[1]
    me = lax.axis_index("dom")
    gather_slots(places, pieces, values)
    row = jnp.concatenate(
        [halo[pl.ds(jnp.bitwise_xor(me, r), 1), :] for r in range(doms)], axis=1
    )
    parts = [row[:, 128 * k : 128 * (k + 1)] for k in range(row.shape[1] // 128)]
    out[...] = (
        node_grad[...]
        + mm(pick_columns(parts, out.shape[0]), values[...])
        + mm_nt(near[...], weights[width : 2 * width, :])
        + mm_nt(recv_total[...], weights[2 * width : 3 * width, :])
    ).astype(BF16)


def coarse_final_kernel(chips, scale, mine, other, out):
    step = mine.shape[0] // (4 * chips)
    rows = out.shape[0] // (8 * chips)
    core = my_core()
    chip = lax.axis_index("grp") // 2
    place = coarse_place()
    for which, ref in ((0, mine), (1, other)):
        for c in range(chips):
            member = jnp.bitwise_xor(core, which) * chips + jnp.bitwise_xor(chip, c)
            for r in range(4):
                first = (member * 4 + jnp.bitwise_xor(place, r)) * rows
                here = (c * 4 + r) * step
                out[pl.ds(pl.multiple_of(first, 8), rows), :] = (
                    ref[here : here + rows, :].astype(F32) * scale
                )


def fine_final_kernel(scale, edge_mine, edge_other, node_mine, node_other, out):
    width = out.shape[1]
    place = fine_place()
    rows = 4 * width // 16
    node_rows = 3 * width // 16
    step = node_mine.shape[0] // 8
    for r in range(16):
        at = jnp.bitwise_xor(place, r)
        here = slice((r % 8) * rows, (r % 8 + 1) * rows)
        out[pl.ds(pl.multiple_of(at * rows, 16), rows), :] = (
            (edge_mine, edge_other)[r // 8][here, :].astype(F32) * scale
        )
        end = (r % 8 + 1) * step
        first = pl.multiple_of(4 * width + at * node_rows, 16)
        out[pl.ds(first, node_rows), :] = (
            (node_mine, node_other)[r // 8][end - node_rows : end, :].astype(F32) * scale
        )


def swap_core(value, groups):
    return lax.ppermute(value, "grp", [(i, i ^ 1) for i in range(groups)])


def turn_chip(value, groups, places):
    return lax.ppermute(
        value, "grp", [(i, (i + 2 * places) % groups) for i in range(groups)]
    )


def group_rest(own, scale, groups):
    sent = own.astype(BF16)
    for k in range(1, groups // 2):
        own = own + turn_chip(sent, groups, k).astype(F32)
    return (own * scale).astype(BF16)


def pair_sum(mine, other, groups):
    return mine.astype(F32) + swap_core(other, groups).astype(F32)


def flip(value, axis, bit):
    size = lax.axis_size(axis)
    return lax.ppermute(value, axis, [(i, i ^ (1 << bit)) for i in range(size)])


def add(a, b):
    return (a.astype(F32) + b.astype(F32)).astype(BF16)


def halved(values):
    half = values.shape[0] // 2
    return values[:half], values[half:]


def exchange_slots(near, far, slots):
    doms = lax.axis_size("dom")
    arrays = [near]
    places = [(0, r) for r in range(doms // 2)] + [None] * (doms // 2)
    for bit in reversed(range(doms.bit_length() - 1)):
        moved_slots = [r for r in range(doms) if r >> bit & 1]
        if bit == doms.bit_length() - 2:
            sent = far
        else:
            sent = jnp.concatenate(
                [arrays[w][slot * slots : (slot + 1) * slots] for w, slot in
                 (places[r] for r in moved_slots)],
                axis=0,
            )
        arrays.append(flip(sent, "dom", bit))
        for i, r in enumerate(moved_slots):
            places[r] = (len(arrays) - 1, i)
    return arrays, places


def body(
    nodes,
    edges,
    senders,
    receivers,
    edge_count,
    halo_rows,
    aggregates,
    coarse_edges,
    coarse_senders,
    coarse_receivers,
    cotangent,
    fine_weights,
    coarse_weights,
):
    node_count, width = nodes.shape
    edge_total = edges.shape[0]
    groups = lax.axis_size("grp")
    domains = lax.axis_size("dom")
    devices = groups * domains
    chips = groups // 2
    group_rows = ROWS * groups
    slots = halo_rows.shape[2]
    halo_count = domains * slots
    coarse_total = coarse_senders.shape[1]
    tiles = node_count // ROWS
    tile = edge_total // tiles
    step_edges = 2 * tile
    steps = tiles // 2

    halo_index = halo_rows[0]
    sender_rows = senders.reshape(-1, 128)
    receiver_rows = receivers.reshape(-1, 128)
    aggregate_rows = aggregates.reshape(-1, 128)
    half = shape(group_rows // 2, width)

    def call(kernel, name, micros, outs, ins, scratch=(), limit=20, specs=None, grid=None):
        outs = tuple(outs)
        in_specs, out_specs = specs or (
            [
                smem() if len(leaf.shape) == 1 else pl.BlockSpec(memory_space=pltpu.VMEM)
                for leaf in ins
            ],
            [pl.BlockSpec(memory_space=pltpu.VMEM) for leaf in outs],
        )
        result = kernel_call(
            kernel,
            micros,
            limit,
            out_shape=outs,
            in_specs=in_specs,
            out_specs=out_specs,
            scratch_shapes=list(scratch),
            name=name,
            **({} if grid is None else {"grid": (grid,)}),
        )(*ins)
        return result[0] if len(outs) == 1 else result

    def streamed(kernel, name, micros, outs, ins, scratch=(), limit=20):
        specs = ([whole(leaf) for leaf in ins], [whole(leaf) for leaf in outs])
        return call(kernel, name, micros, outs, ins, scratch, limit, specs, 1)

    def room(rows, columns=width, dtype=BF16):
        return pltpu.VMEM((rows, columns), dtype)

    send_near, send_far = streamed(
        send_kernel, "send_rows", 2,
        [shape(halo_count // 2, width), shape(halo_count // 2, width)], [nodes, halo_index],
    )
    send_far, later_cotangent = lax.optimization_barrier((send_far, cotangent))
    incoming, places = exchange_slots(send_near, send_far, slots)
    cot_mine, cot_other = call(
        cotangent_kernel, "cotangent_sums", 1, [half, half], [aggregate_rows, later_cotangent],
        scratch=[room(group_rows)],
    )
    cot_pair = pair_sum(cot_mine, cot_other, groups)

    partial = call(
        functools.partial(fine_local_kernel, tile, step_edges), "fine_local", 5,
        [shape(edge_total, width)],
        [edge_count, edges, sender_rows, receiver_rows, nodes, fine_weights],
        scratch=[room(node_count), room(node_count), room(step_edges, node_count)],
    )
    partial, cot_pair = lax.optimization_barrier((partial, cot_pair))
    cot_own = group_rest(cot_pair, 1.0, groups)
    per_edge = shape(edge_total, width)
    per_node = shape(node_count, width)
    halo_outs = [
        per_edge, per_edge, per_edge, shape(edge_total, 1, F32), per_node, per_node, per_node,
        shape(node_count, 1, F32), per_node, per_node, half, half, shape(halo_count, width),
    ]
    halo_ins = [
        edge_count, partial, sender_rows, receiver_rows, aggregate_rows, nodes, fine_weights,
        *incoming,
    ]
    (
        active, slope, unit, scale, node_active, node_slope, node_unit, node_scale, summed,
        refined, part_mine, part_other, halo_nodes,
    ) = call(
        functools.partial(fine_halo_kernel, tile, places), "fine_halo", 7, halo_outs, halo_ins,
        scratch=[
            room(halo_count),
            room(step_edges, halo_count),
            room(step_edges, width, F32),
            room(step_edges, width, F32),
            room(group_rows),
        ],
        limit=24,
        specs=(
            [smem(), by_tile(step_edges, width)] + [whole(leaf) for leaf in halo_ins[2:]],
            [by_tile(step_edges, leaf.shape[1]) for leaf in halo_outs[:4]]
            + [whole(leaf) for leaf in halo_outs[4:]],
        ),
        grid=steps,
    )
    part_mine, part_other, cot_own = lax.optimization_barrier((part_mine, part_other, cot_own))
    table_own = group_rest(pair_sum(part_mine, part_other, groups), 0.125, groups)
    tables = [table_own, swap_core(table_own, groups)]
    cots = [cot_own, swap_core(cot_own, groups)]

    coarse_chunk = 2 * coarse_total // groups
    share = 7 * width // groups
    coarse_table, table_grad, coarse_mine, coarse_other = call(
        functools.partial(coarse_kernel, groups, coarse_chunk), "coarse_both_ways", 8,
        [shape(group_rows, width), shape(group_rows, width)] + [shape(share // 2, width)] * 2,
        [
            *tables, *cots, coarse_edges[0], coarse_senders.reshape(-1, 128),
            coarse_receivers.reshape(-1, 128), coarse_weights,
        ],
        scratch=[room(group_rows)] * 12
        + [room(coarse_total)] * 3
        + [room(coarse_total, 1, F32)]
        + [room(coarse_total)] * 2
        + [room(coarse_chunk, group_rows)]
        + [room(max(coarse_chunk, group_rows), width, F32)] * 2
        + [room(group_rows, 1, F32), room(group_rows, width, F32), room(7 * width, width, F32)],
        limit=28,
    )
    half_nodes = shape(3 * width // 2, width)
    node_partial, summed_grad, node_mine, node_other = call(
        node_back_kernel, "node_back", 5,
        [shape(node_count, width, F32), per_node, half_nodes, half_nodes],
        [
            aggregate_rows, table_grad, cotangent, node_active, node_slope, node_unit, node_scale,
            summed, nodes, fine_weights,
        ],
        scratch=[room(node_count)] * 2 + [room(node_count, width, F32)] * 2 + [room(3 * width)],
    )
    fine_out = streamed(
        fine_out_kernel, "fine_out", 2, [per_node], [aggregate_rows, coarse_table, refined]
    )
    more_grp = range(2, groups.bit_length() - 1)
    more_dom = range(2, domains.bit_length() - 1)

    def early_sum():
        mine, other = node_mine, node_other
        for bit in (0, 1):
            received = yield flip(other, "grp", bit)
            mine, other = halved(add(mine, received))
        own = jnp.concatenate([mine, other], axis=0)
        for bit in more_grp:
            own = add(own, (yield flip(own, "grp", bit)))
        n = own.shape[0] // 4
        c = share // 4
        mine, other = (
            jnp.concatenate(
                [
                    coarse[:c], own[2 * k * n : (2 * k + 1) * n],
                    coarse[c:], own[(2 * k + 1) * n : (2 * k + 2) * n],
                ],
                axis=0,
            )
            for k, coarse in enumerate((coarse_mine, coarse_other))
        )
        received = yield flip(other, "dom", 0)
        mine, other = halved(add(mine, received))
        own = add(mine, (yield flip(other, "dom", 1)))
        for bit in more_dom:
            own = add(own, (yield flip(own, "dom", bit)))
        for bit in (1, 0):
            own = jnp.concatenate([own, (yield flip(own, "dom", bit))], axis=0)
        for bit in range(1, groups.bit_length() - 1):
            own = jnp.concatenate([own, (yield flip(own, "grp", bit))], axis=0)
        return own

    early = early_sum()
    moving = next(early)
    moving, summed_grad, fine_out = lax.optimization_barrier((moving, summed_grad, fine_out))

    sources = node_count + halo_count
    square = shape(width, width, F32)
    edge_ins = [
        edge_count, edges, active, slope, unit, scale, sender_rows, receiver_rows, summed_grad,
        fine_weights,
    ]
    edge_room = [room(step_edges), room(step_edges, width, F32), room(step_edges, width, F32)]
    step_shape = shape(step_edges, width)
    recv_shape = shape(node_count // steps, width)
    half_weights = shape(2 * width, width)
    hidden_grads, recv_sums, sums = [], [], []
    for part in range(steps):
        moving = early.send(moving)
        last = part == steps - 1
        kernel = functools.partial(edge_back_kernel, part, last, tile, slots, step_edges)
        if last:
            (
                hidden_grad, near, recv_total, weight_mine, weight_other, halo_near, halo_far
            ) = call(
                kernel, "edge_back_%d" % part, 3,
                [step_shape, per_node, per_node, half_weights, half_weights]
                + [shape(halo_count // 2, width)] * 2,
                edge_ins + sums + [nodes, halo_nodes] + recv_sums,
                scratch=[
                    room(node_count // steps),
                    room(sources, width, F32),
                    room(width, width, F32),
                    room(width, width, F32),
                ]
                + edge_room
                + [room(4 * width)],
            )
            moving, weight_mine, weight_other = lax.optimization_barrier(
                (moving, weight_mine, weight_other)
            )
        else:
            hidden_grad, recv_sum, *sums = call(
                kernel, "edge_back_%d" % part, 2,
                [step_shape, recv_shape, shape(sources, width, F32), square, square],
                edge_ins + sums,
                scratch=edge_room,
            )
            recv_sums.append(recv_sum)
            moving, *sums = lax.optimization_barrier((moving, *sums))
        hidden_grads.append(hidden_grad)

    mine, other = halved(add(weight_mine, flip(weight_other, "grp", 0)))
    other, halo_near, halo_far, *hidden_grads = lax.optimization_barrier(
        (other, halo_near, halo_far, *hidden_grads)
    )
    edge_grad = call(
        edge_out_kernel, "edge_out", 3, [per_edge], [fine_weights, *hidden_grads],
        specs=(
            [whole(fine_weights)] + [whole(leaf) for leaf in hidden_grads],
            [by_tile(step_edges, width)],
        ),
        grid=steps,
    )
    returned, places_back = exchange_slots(halo_near, halo_far, slots)
    received = flip(other, "grp", 1)
    received, edge_grad = lax.optimization_barrier((received, edge_grad))
    mine, other = halved(add(mine, received))
    mine, other = halved(add(mine, flip(other, "dom", 0)))
    own = add(mine, flip(other, "dom", 1))
    for axis, bits in (("grp", more_grp), ("dom", more_dom)):
        for bit in bits:
            own = add(own, flip(own, axis, bit))

    while True:
        try:
            moving = early.send(moving)
        except StopIteration as stop:
            early_mine = stop.value
            break
    early_other = flip(early_mine, "grp", 0)
    weight_shape = shape(7 * width, width, F32)
    coarse_total_grad = streamed(
        functools.partial(coarse_final_kernel, chips, (coarse_total * domains) ** (-0.5)),
        "coarse_weights", 2, [weight_shape], [early_mine, early_other],
    )
    node_grad = streamed(
        functools.partial(return_kernel, places_back), "halo_return", 3, [per_node],
        [halo_index, node_partial, near, recv_total, fine_weights, *returned],
        scratch=[room(halo_count)],
    )
    for axis, bit in (("dom", 1), ("dom", 0)):
        own = jnp.concatenate([own, flip(own, axis, bit)], axis=0)
    own, node_grad = lax.optimization_barrier((own, node_grad))
    own = jnp.concatenate([own, flip(own, "grp", 1)], axis=0)
    own, coarse_total_grad = lax.optimization_barrier((own, coarse_total_grad))
    eight = (early_mine.shape[0] // chips) * 2
    fine_total_grad = streamed(
        functools.partial(fine_final_kernel, (edge_total * devices) ** (-0.5)),
        "fine_weights", 2, [weight_shape],
        [own, flip(own, "grp", 0), early_mine[:eight], early_other[:eight]],
    )
    return (fine_out, node_grad, edge_grad, fine_total_grad, coarse_total_grad)


def solution(mesh):
    placed = (
        P(("dom", "grp"), None),
        P(("dom", "grp"), None),
        P(("dom", "grp")),
        P(("dom", "grp")),
        P(("dom", "grp")),
        P(("dom", "grp"), None, None),
        P(("dom", "grp")),
        P("dom", None, None),
        P("dom", None),
        P("dom", None),
        P(("dom", "grp"), None),
        P(),
        P(),
    )
    return jax.shard_map(
        body,
        mesh=mesh,
        in_specs=placed,
        out_specs=(
            P(("dom", "grp"), None),
            P(("dom", "grp"), None),
            P(("dom", "grp"), None),
            P(),
            P(),
        ),
        check_vma=False,
    )
```

```python
import functools

import jax
import jax.numpy as jnp
from jax import lax
from jax.experimental import pallas as pl
from jax.experimental.pallas import tpu as pltpu
from jax.sharding import PartitionSpec as P

F32 = jnp.float32
BF16 = jnp.bfloat16
ROWS = 128
MIB = 1024 * 1024
CHUNK = 64
I16 = jnp.int16


def mm(a, b):
    return lax.dot_general(a, b, (((1,), (0,)), ((), ())), preferred_element_type=F32)


def mm_nt(a, b):
    return lax.dot_general(a, b, (((1,), (1,)), ((), ())), preferred_element_type=F32)


def mm_tn(a, b):
    return lax.dot_general(a, b, (((0,), (0,)), ((), ())), preferred_element_type=F32)


def column(row):
    return jnp.broadcast_to(row, (128, row.shape[1])).T.astype(I16)


def flags(mask):
    return jnp.where(mask, jnp.ones((), BF16), jnp.zeros((), BF16))


def pick_rows(rows, width):
    lane = lax.broadcasted_iota(jnp.int32, (rows[0].shape[1], 128), 1).astype(I16)
    out = []
    for row in rows:
        index = column(row)
        out.append(
            jnp.concatenate([flags(index == lane + I16(128 * k)) for k in range(width // 128)], axis=1)
        )
    return out[0] if len(out) == 1 else jnp.concatenate(out, axis=0)


def pick_columns(rows, height):
    sub = lax.broadcasted_iota(jnp.int32, (height, rows[0].shape[1]), 0).astype(I16)
    out = []
    for row in rows:
        index = jnp.broadcast_to(row, (16, row.shape[1])).astype(I16)
        out.append(flags(sub == jnp.broadcast_to(index[0:1, :], sub.shape)))
    return out[0] if len(out) == 1 else jnp.concatenate(out, axis=1)


def gate(hidden):
    return 0.5 + 0.5 * jnp.tanh(0.5 * hidden)


def normalise(values):
    centre = values - jnp.mean(values, axis=-1, keepdims=True)
    spread = jnp.mean(centre * centre, axis=-1, keepdims=True)
    scale = lax.rsqrt(spread + 1e-05)
    return centre * scale, scale


def normalise_back(grad, unit, scale):
    along = jnp.mean(grad * unit, axis=-1, keepdims=True)
    return scale * (grad - jnp.mean(grad, axis=-1, keepdims=True) - unit * along)


def kernel_call(kernel, micros, limit, **kwargs):
    return pl.pallas_call(
        kernel,
        compiler_params=pltpu.CompilerParams(vmem_limit_bytes=limit * MIB),
        cost_estimate=pl.CostEstimate(
            flops=int(micros * 1.1e9), bytes_accessed=1 << 20, transcendentals=0
        ),
        **kwargs,
    )


def smem():
    return pl.BlockSpec(memory_space=pltpu.SMEM)


def whole(array):
    return pl.BlockSpec(array.shape, lambda t: (0,) * len(array.shape))


def by_tile(rows, columns):
    return pl.BlockSpec((rows, columns), lambda t: (t, 0))


def shape(rows, columns, dtype=BF16):
    return jax.ShapeDtypeStruct((rows, columns), dtype)


def chunks(total):
    return [slice(r, r + CHUNK) for r in range(0, total, CHUNK)]


def spans(start, size, tile):
    return [
        (
            slice(at, at + tile),
            slice(start + at, start + at + tile),
            slice((start + at) // tile * ROWS, ((start + at) // tile + 1) * ROWS),
        )
        for at in range(0, size, tile)
    ]


def at(start, here):
    return slice(start + here.start, start + here.stop)


def staggered(count, *stages):
    for t in range(count + len(stages) - 1):
        for k, stage in enumerate(stages):
            if 0 <= t - k < count:
                stage(t - k)


def my_core():
    return lax.rem(lax.axis_index("grp"), 2)


def split_halves(ref, mine_out, other_out):
    half = mine_out.shape[0]
    core = my_core()
    mine_out[...] = ref[pl.ds(core * half, half), :]
    other_out[...] = ref[pl.ds((1 - core) * half, half), :]


def one_hot_kernel(tile, node_count, slots, count, senders, receivers, far_out, rows_out, columns_out):
    lane = lax.broadcasted_iota(jnp.int32, (1, 128), 1)
    mask = lax.axis_index("dom") * slots
    for j in range(senders.shape[0]):
        here = slice(j * 128, (j + 1) * 128)
        row = jnp.bitwise_xor(senders[j : j + 1, :] - node_count, mask)
        far_out[here, :] = pick_rows([row], far_out.shape[1])
        row = receivers[j : j + 1, :] - j * 128 // tile * ROWS
        row = jnp.where(lane + j * 128 % tile < count[0], row, -1)
        rows_out[here, :] = pick_rows([row], ROWS)
        columns_out[:, here] = pick_columns([row], ROWS)


def sender_kernel(node_count, slots, senders, columns_out):
    mask = lax.axis_index("dom") * slots
    for j in range(senders.shape[0]):
        row = senders[j : j + 1, :]
        row = jnp.where(
            row < node_count, row, jnp.bitwise_xor(row - node_count, mask) + node_count
        )
        columns_out[:, j * 128 : (j + 1) * 128] = pick_columns([row], columns_out.shape[0])


def send_kernel(nodes, halo, near_out, far_out):
    doms, slots = halo.shape
    me = lax.axis_index("dom")
    for first, out in ((0, near_out), (doms // 2, far_out)):
        picks = [
            pick_rows([halo[pl.ds(jnp.bitwise_xor(me, first + r), 1), :]], nodes.shape[0])
            for r in range(doms // 2)
        ]
        out[...] = mm(jnp.concatenate(picks, axis=0), nodes[...]).astype(BF16)


def gather_slots(places, refs, out):
    slots = out.shape[0] // len(places)
    for r, (which, slot) in enumerate(places):
        out[r * slots : (r + 1) * slots, :] = refs[which][slot * slots : (slot + 1) * slots, :]


def group_sums(aggregates, values, mine_out, other_out, sums):
    rows = [aggregates[k : k + 1, :] for k in range(aggregates.shape[0])]
    sums[...] = mm(pick_columns(rows, sums.shape[0]), values).astype(BF16)
    split_halves(sums, mine_out, other_out)


def cotangent_kernel(aggregates, cotangent, mine_out, other_out, sums):
    group_sums(aggregates, cotangent[...], mine_out, other_out, sums)


def fine_local_kernel(
    tile, step_edges, edges, senders, recv_rows, nodes, weights,
    partial_out, send_proj, recv_proj, pick,
):
    width = nodes.shape[1]
    parts = step_edges // 128
    send_proj[...] = mm(nodes[...], weights[width : 2 * width, :]).astype(BF16)
    recv_proj[...] = mm(nodes[...], weights[2 * width : 3 * width, :]).astype(BF16)

    def choose(i):
        for j in range(parts):
            row = senders[i * parts + j : i * parts + j + 1, :]
            pick[i % 2, j * 128 : (j + 1) * 128, :] = pick_rows([row], nodes.shape[0])

    def multiply(i):
        for here, there, own in spans(i * step_edges, step_edges, tile):
            partial_out[there, :] = (
                mm(edges[there, :], weights[:width, :])
                + mm(recv_rows[there, :], recv_proj[own, :])
                + mm(pick[i % 2, here, :], send_proj[...])
            ).astype(BF16)

    staggered(edges.shape[0] // step_edges, choose, multiply)


def activate(hidden, active_out, slope_out, here):
    opened = gate(hidden)
    active = hidden * opened
    active_out[here, :] = active.astype(BF16)
    slope_out[here, :] = (opened + active * (1.0 - opened)).astype(BF16)


def fine_halo_kernel(
    tile, step_edges, places, partial, far_rows, recv_columns, aggregates, nodes, weights, *refs
):
    pieces = refs[: -(13 + 4)]
    (
        active_out, slope_out, unit_out, scale_out,
        node_active_out, node_slope_out, node_unit_out, node_scale_out, summed_out, refined_out,
        mine_out, other_out, halo,
        halo_proj, wide, wide_next, sums,
    ) = refs[-(13 + 4) :]
    node_count, width = nodes.shape
    gather_slots(places, pieces, halo)
    halo_proj[...] = mm(halo[...], weights[width : 2 * width, :]).astype(BF16)

    def first(i):
        start = i * step_edges
        wide[i % 2] = mm(far_rows[start : start + step_edges, :], halo_proj[...])
        for here in chunks(step_edges):
            there = at(start, here)
            activate(
                partial[there, :].astype(F32) + wide[i % 2, here, :], active_out, slope_out, there
            )

    def second(i):
        start = i * step_edges
        wide_next[i % 2] = mm(
            active_out[start : start + step_edges, :], weights[3 * width : 4 * width, :]
        )
        for here in chunks(step_edges):
            there = at(start, here)
            unit, scale = normalise(wide_next[i % 2, here, :])
            unit_out[there, :] = unit.astype(BF16)
            scale_out[there, :] = scale
        for here, there, own in spans(start, step_edges, tile):
            summed_out[own, :] = mm(recv_columns[:, there], unit_out[there, :]).astype(BF16)

    staggered(partial.shape[0] // step_edges, first, second)

    wide[0] = mm(nodes[...], weights[4 * width : 5 * width, :]) + mm(
        summed_out[...], weights[5 * width : 6 * width, :]
    )
    for here in chunks(node_count):
        activate(wide[0, here, :], node_active_out, node_slope_out, here)
    wide_next[0] = mm(node_active_out[...], weights[6 * width :, :])
    for here in chunks(node_count):
        unit, scale = normalise(wide_next[0, here, :])
        node_unit_out[here, :] = unit.astype(BF16)
        node_scale_out[here, :] = scale
        refined_out[here, :] = (nodes[here, :].astype(F32) + unit).astype(BF16)
    group_sums(aggregates, refined_out[...], mine_out, other_out, sums)


def coarse_pre_kernel(
    groups, edges, senders, receivers, weights,
    partial_out, send_rows_out, send_columns_out, recv_rows_out, recv_columns_out,
):
    total, width = edges.shape
    group_rows = send_columns_out.shape[0]
    tile = total // groups
    partial_out[...] = mm(edges[...], weights[:width, :]).astype(BF16)

    def run(i, carry):
        for j in range(tile // 128):
            at = i * (tile // 128) + j
            there = pl.ds(pl.multiple_of(at * 128, 128), 128)
            send, recv = senders[pl.ds(at, 1), :], receivers[pl.ds(at, 1), :]
            send_rows_out[there, :] = pick_rows([send], group_rows)
            recv_rows_out[there, :] = pick_rows([recv], ROWS)
            send_columns_out[:, there] = pick_columns([send], group_rows)
            recv_columns_out[:, there] = pick_columns([recv], ROWS)
        return carry

    lax.fori_loop(0, groups, run, 0)


def coarse_kernel(
    groups, chunk,
    table_mine, table_other, cot_mine, cot_other, partial, send_rows, send_columns, recv_rows,
    recv_columns, weights,
    table, output_out, grad_out, summed, node_active, node_pre, node_hidden_grad, send_total,
    recv_sum, active_all, hidden_grad_all, pre_all,
    cot, send_proj, recv_proj, summed_grad, node_slope, node_unit,
    slope_all, unit_all, scale_all, wide, wide_next, own_grad, send_sum,
):
    group_rows, width = table.shape
    half = group_rows // 2
    total = partial.shape[0]
    tile = total // groups
    spans = chunk // tile
    steps = total // chunk
    core = my_core()
    mine = pl.ds(core * half, half)
    other = pl.ds((1 - core) * half, half)
    table[mine, :] = table_mine[...]
    table[other, :] = table_other[...]
    cot[mine, :] = cot_mine[...]
    cot[other, :] = cot_other[...]
    send_proj[...] = mm(table[...], weights[width : 2 * width, :]).astype(BF16)
    recv_proj[...] = mm(table[...], weights[2 * width : 3 * width, :]).astype(BF16)

    def places(i):
        start = i * chunk
        return [
            (
                slice(s * tile, (s + 1) * tile),
                pl.ds(start + s * tile, tile),
                pl.ds((i * spans + s) * ROWS, ROWS),
            )
            for s in range(spans)
        ]

    for i in range(steps):
        start = i * chunk
        all_here = slice(start, start + chunk)
        for here, there, own in places(i):
            wide[here, :] = mm(send_rows[there, :], send_proj[...]) + mm(
                recv_rows[there, :], recv_proj[own, :]
            )
        for here in chunks(chunk):
            there = slice(start + here.start, start + here.stop)
            activate(
                wide[here, :] + partial[there, :].astype(F32), active_all, slope_all, there
            )
        wide_next[...] = mm(active_all[all_here, :], weights[3 * width : 4 * width, :])
        for here in chunks(chunk):
            there = slice(start + here.start, start + here.stop)
            unit, scale = normalise(wide_next[here, :])
            unit_all[there, :] = unit.astype(BF16)
            scale_all[there, :] = scale
        for here, there, own in places(i):
            summed[own, :] = mm(recv_columns[:, there], unit_all[there, :]).astype(BF16)

    nodes_here = slice(0, group_rows)
    wide[nodes_here, :] = mm(table[...], weights[4 * width : 5 * width, :]) + mm(
        summed[...], weights[5 * width : 6 * width, :]
    )
    for here in chunks(group_rows):
        activate(wide[here, :], node_active, node_slope, here)
    wide_next[nodes_here, :] = mm(node_active[...], weights[6 * width :, :])
    for here in chunks(group_rows):
        unit, scale = normalise(wide_next[here, :])
        output_out[here, :] = (table[here, :].astype(F32) + unit).astype(BF16)
        node_pre[here, :] = normalise_back(cot[here, :].astype(F32), unit, scale).astype(BF16)
    wide[nodes_here, :] = mm_nt(node_pre[...], weights[6 * width :, :])
    for here in chunks(group_rows):
        node_hidden_grad[here, :] = (wide[here, :] * node_slope[here, :].astype(F32)).astype(BF16)
    summed_grad[...] = mm_nt(
        node_hidden_grad[...], weights[5 * width : 6 * width, :]
    ).astype(BF16)
    own_grad[...] = mm_nt(node_hidden_grad[...], weights[4 * width : 5 * width, :])

    for i in range(steps):
        start = i * chunk
        all_here = slice(start, start + chunk)
        for here, there, own in places(i):
            wide[here, :] = mm(recv_rows[there, :], summed_grad[own, :])
        for here in chunks(chunk):
            there = slice(start + here.start, start + here.stop)
            pre_all[there, :] = normalise_back(
                wide[here, :], unit_all[there, :].astype(F32), scale_all[there, :]
            ).astype(BF16)
        wide_next[...] = mm_nt(pre_all[all_here, :], weights[3 * width : 4 * width, :])
        for here in chunks(chunk):
            there = slice(start + here.start, start + here.stop)
            hidden_grad_all[there, :] = (
                wide_next[here, :] * slope_all[there, :].astype(F32)
            ).astype(BF16)
        for here, there, own in places(i):
            recv_sum[own, :] = mm(recv_columns[:, there], hidden_grad_all[there, :]).astype(BF16)
        sent = mm(send_columns[:, all_here], hidden_grad_all[all_here, :])
        if i == 0:
            send_sum[...] = sent
        else:
            send_sum[...] += sent

    send_total[...] = send_sum[...].astype(BF16)
    grad_out[...] = (
        cot[...].astype(F32)
        + own_grad[...]
        + mm_nt(send_total[...], weights[width : 2 * width, :])
        + mm_nt(recv_sum[...], weights[2 * width : 3 * width, :])
    ).astype(BF16)


def coarse_products_kernel(
    groups, edges, table, summed, node_active, node_pre, node_hidden_grad, send_total, recv_total,
    active_all, hidden_grad_all, pre_all,
    weight_mine, weight_other,
    weight_all,
):
    width = table.shape[1]
    share = weight_mine.shape[0] * 2
    begin = (my_core() * (groups // 2) + lax.axis_index("grp") // 2) * share
    products = [
        (edges, hidden_grad_all),
        (table, send_total),
        (table, recv_total),
        (active_all, pre_all),
        (table, node_hidden_grad),
        (summed, node_hidden_grad),
        (node_active, node_pre),
    ]
    for b, (left, right) in enumerate(products):

        @pl.when((b * width < begin + share) & ((b + 1) * width > begin))
        def _():
            weight_all[b * width : (b + 1) * width, :] = mm_tn(left[...], right[...])

    chunk_rows = share // 4
    place = coarse_place()
    for r in range(4):
        first = pl.multiple_of(begin + jnp.bitwise_xor(place, r) * chunk_rows, 8)
        out = (weight_mine, weight_other)[r // 2]
        here = slice((r % 2) * chunk_rows, (r % 2 + 1) * chunk_rows)
        out[here, :] = weight_all[pl.ds(first, chunk_rows), :].astype(BF16)


def coarse_place():
    dom = lax.axis_index("dom")
    return lax.rem(dom, 2) * 2 + lax.rem(dom // 2, 2)


def fine_place():
    grp = lax.axis_index("grp")
    return lax.rem(grp, 2) * 8 + lax.rem(grp // 2, 2) * 4 + coarse_place()


def node_back_kernel(
    aggregates, table_grad, cotangent, node_active, node_slope, node_unit, node_scale, summed,
    nodes, weights,
    node_grad_out, summed_grad_out, weight_out,
    pre, hidden_grad, wide, wide_next,
):
    node_count, width = nodes.shape
    rows = [aggregates[k : k + 1, :] for k in range(aggregates.shape[0])]
    wide[...] = mm(pick_rows(rows, table_grad.shape[0]), table_grad[...])
    for here in chunks(node_count):
        grad = (cotangent[here, :].astype(F32) + 0.125 * wide[here, :]).astype(BF16)
        grad = grad.astype(F32)
        node_grad_out[here, :] = grad
        pre[here, :] = normalise_back(
            grad, node_unit[here, :].astype(F32), node_scale[here, :]
        ).astype(BF16)
    wide_next[...] = mm_nt(pre[...], weights[6 * width :, :])
    for here in chunks(node_count):
        hidden_grad[here, :] = (
            wide_next[here, :] * node_slope[here, :].astype(F32)
        ).astype(BF16)
    summed_grad_out[...] = mm_nt(
        hidden_grad[...], weights[5 * width : 6 * width, :]
    ).astype(BF16)
    node_grad_out[...] += mm_nt(hidden_grad[...], weights[4 * width : 5 * width, :])
    weight_out[:width, :] = mm_tn(nodes[...], hidden_grad[...]).astype(BF16)
    weight_out[width : 2 * width, :] = mm_tn(summed[...], hidden_grad[...]).astype(BF16)
    weight_out[2 * width :, :] = mm_tn(node_active[...], pre[...]).astype(BF16)


def edge_back_kernel(
    tile, step_edges, edges, active, slope, unit, scale, send_columns, recv_rows, recv_columns,
    summed_grad, weights, nodes, halo, node_weights,
    hidden_grad_out, near_out, recv_sum, weight_mine, weight_other, halo_near, halo_far,
    pre, wide, wide_next, weight_all,
):
    node_count, width = nodes.shape

    def first(i):
        start = i * step_edges
        for here, there, own in spans(start, step_edges, tile):
            wide[i % 2, here, :] = mm(recv_rows[there, :], summed_grad[own, :])
        for here in chunks(step_edges):
            there = at(start, here)
            pre[there, :] = normalise_back(
                wide[i % 2, here, :], unit[there, :].astype(F32), scale[there, :]
            ).astype(BF16)

    def second(i):
        start = i * step_edges
        wide_next[i % 2] = mm_nt(
            pre[start : start + step_edges, :], weights[3 * width : 4 * width, :]
        )
        for here in chunks(step_edges):
            there = at(start, here)
            hidden_grad_out[there, :] = (
                wide_next[i % 2, here, :] * slope[there, :].astype(F32)
            ).astype(BF16)

    staggered(edges.shape[0] // step_edges, first, second)

    hidden_grad = hidden_grad_out[...]
    near_out[...] = mm(send_columns[:node_count, :], hidden_grad).astype(BF16)
    far = mm(send_columns[node_count:, :], hidden_grad).astype(BF16)
    for here, there, own in spans(0, edges.shape[0], tile):
        recv_sum[own, :] = mm(recv_columns[:, there], hidden_grad_out[there, :]).astype(BF16)
    weight_all[3 * width : 4 * width, :] = mm_tn(active[...], pre[...])
    weight_all[:width, :] = mm_tn(edges[...], hidden_grad)
    weight_all[width : 2 * width, :] = mm_tn(nodes[...], near_out[...]) + mm_tn(halo[...], far)
    weight_all[2 * width : 3 * width, :] = mm_tn(nodes[...], recv_sum[...])
    weight_all[4 * width :, :] = node_weights[...].astype(F32)
    far_half = far.shape[0] // 2
    send_weights = weights[width : 2 * width, :]
    halo_near[...] = mm_nt(far[:far_half, :], send_weights).astype(BF16)
    halo_far[...] = mm_nt(far[far_half:, :], send_weights).astype(BF16)
    rows = weight_all.shape[0] // 16
    place = fine_place()
    for r in range(16):
        begin = pl.multiple_of(jnp.bitwise_xor(place, r) * rows, 16)
        out = (weight_mine, weight_other)[r // 8]
        out[(r % 8) * rows : (r % 8 + 1) * rows, :] = weight_all[pl.ds(begin, rows), :].astype(
            BF16
        )


def edge_out_kernel(hidden_grad, weights, edge_grad_out):
    edge_grad_out[...] = mm_nt(hidden_grad[...], weights[: hidden_grad.shape[1], :]).astype(BF16)


def fine_out_kernel(aggregates, table, refined, fine_out):
    rows = [aggregates[k : k + 1, :] for k in range(aggregates.shape[0])]
    lifted = mm(pick_rows(rows, table.shape[0]), table[...])
    fine_out[...] = (refined[...].astype(F32) + lifted).astype(BF16)


def return_kernel(places, halo, node_grad, near, recv_total, weights, *refs):
    doms = len(places)
    pieces, out, values = refs[:-2], refs[-2], refs[-1]
    width = out.shape[1]
    me = lax.axis_index("dom")
    gather_slots(places, pieces, values)
    row = jnp.concatenate(
        [halo[pl.ds(jnp.bitwise_xor(me, r), 1), :] for r in range(doms)], axis=1
    )
    parts = [row[:, 128 * k : 128 * (k + 1)] for k in range(row.shape[1] // 128)]
    out[...] = (
        node_grad[...]
        + mm(pick_columns(parts, out.shape[0]), values[...])
        + mm_nt(near[...], weights[width : 2 * width, :])
        + mm_nt(recv_total[...], weights[2 * width : 3 * width, :])
    ).astype(BF16)


def coarse_final_kernel(chips, scale, mine, other, out):
    share = mine.shape[0] // chips
    rows = share // 4
    core = my_core()
    chip = lax.axis_index("grp") // 2
    place = coarse_place()
    for k in range(chips):
        at = lax.rem(chip - k + chips, chips)
        for r in range(4):
            here = slice(k * share + r * rows, k * share + (r + 1) * rows)
            inside = jnp.bitwise_xor(place, r) * rows
            first = pl.multiple_of((core * chips + at) * share + inside, 8)
            second = pl.multiple_of(((1 - core) * chips + at) * share + inside, 8)
            out[pl.ds(first, rows), :] = mine[here, :].astype(F32) * scale
            out[pl.ds(second, rows), :] = other[here, :].astype(F32) * scale


def fine_final_kernel(scale, mine, other, out):
    rows = out.shape[0] // 16
    place = fine_place()
    for r in range(16):
        first = pl.multiple_of(jnp.bitwise_xor(place, r) * rows, 16)
        here = slice((r % 8) * rows, (r % 8 + 1) * rows)
        out[pl.ds(first, rows), :] = (mine, other)[r // 8][here, :].astype(F32) * scale


def swap_core(value, groups):
    return lax.ppermute(value, "grp", [(i, i ^ 1) for i in range(groups)])


def turn_chip(value, groups, places):
    return lax.ppermute(
        value, "grp", [(i, (i + 2 * places) % groups) for i in range(groups)]
    )


def group_rest(own, scale, groups):
    sent = own.astype(BF16)
    for k in range(1, groups // 2):
        own = own + turn_chip(sent, groups, k).astype(F32)
    return (own * scale).astype(BF16)


def pair_sum(mine, other, groups):
    return mine.astype(F32) + swap_core(other, groups).astype(F32)


def flip(value, axis, bit):
    size = lax.axis_size(axis)
    return lax.ppermute(value, axis, [(i, i ^ (1 << bit)) for i in range(size)])


def after(value, *others):
    return lax.optimization_barrier((value, *others))[0]


def add(a, b):
    return (a.astype(F32) + b.astype(F32)).astype(BF16)


def halved(values):
    half = values.shape[0] // 2
    return values[:half], values[half:]


def exchange_slots(near, far, slots, ties=()):
    doms = lax.axis_size("dom")
    arrays = [near]
    places = [(0, r) for r in range(doms // 2)] + [None] * (doms // 2)
    for bit in reversed(range(doms.bit_length() - 1)):
        moved_slots = [r for r in range(doms) if r >> bit & 1]
        if bit == doms.bit_length() - 2:
            sent = far
        else:
            sent = jnp.concatenate(
                [arrays[w][slot * slots : (slot + 1) * slots] for w, slot in
                 (places[r] for r in moved_slots)],
                axis=0,
            )
        stage = len(arrays) - 1
        if stage < len(ties):
            sent = after(sent, ties[stage])
        arrays.append(flip(sent, "dom", bit))
        for i, r in enumerate(moved_slots):
            places[r] = (len(arrays) - 1, i)
    return arrays, places


def body(
    nodes,
    edges,
    senders,
    receivers,
    edge_count,
    halo_rows,
    aggregates,
    coarse_edges,
    coarse_senders,
    coarse_receivers,
    cotangent,
    fine_weights,
    coarse_weights,
):
    node_count, width = nodes.shape
    edge_total = edges.shape[0]
    groups = lax.axis_size("grp")
    domains = lax.axis_size("dom")
    devices = groups * domains
    chips = groups // 2
    group_rows = ROWS * groups
    slots = halo_rows.shape[2]
    halo_count = domains * slots
    coarse_total = coarse_senders.shape[1]
    tiles = node_count // ROWS
    tile = edge_total // tiles
    step_edges = 2 * tile
    steps = tiles // 2

    halo_index = halo_rows[0]
    sender_rows = senders.reshape(-1, 128)
    receiver_rows = receivers.reshape(-1, 128)
    aggregate_rows = aggregates.reshape(-1, 128)
    half = shape(group_rows // 2, width)

    def call(kernel, name, micros, outs, ins, scratch=(), limit=20, specs=None, grid=None):
        outs = tuple(outs)
        in_specs, out_specs = specs or (
            [
                smem() if len(leaf.shape) == 1 else pl.BlockSpec(memory_space=pltpu.VMEM)
                for leaf in ins
            ],
            [pl.BlockSpec(memory_space=pltpu.VMEM) for leaf in outs],
        )
        result = kernel_call(
            kernel,
            micros,
            limit,
            out_shape=outs,
            in_specs=in_specs,
            out_specs=out_specs,
            scratch_shapes=list(scratch),
            name=name,
            **({} if grid is None else {"grid": (grid,)}),
        )(*ins)
        return result[0] if len(outs) == 1 else result

    def streamed(kernel, name, micros, outs, ins, scratch=(), limit=20):
        specs = ([whole(leaf) for leaf in ins], [whole(leaf) for leaf in outs])
        return call(kernel, name, micros, outs, ins, scratch, limit, specs, 1)

    def room(rows, columns=width, dtype=BF16):
        return pltpu.VMEM((rows, columns), dtype)

    send_near, send_far = streamed(
        send_kernel, "send_rows", 2,
        [shape(halo_count // 2, width), shape(halo_count // 2, width)], [nodes, halo_index],
    )
    send_far, later_cotangent = lax.optimization_barrier((send_far, cotangent))
    incoming, places = exchange_slots(send_near, send_far, slots)
    cot_mine, cot_other = call(
        cotangent_kernel, "cotangent_sums", 1, [half, half], [aggregate_rows, later_cotangent],
        scratch=[room(group_rows)],
    )
    cot_pair = pair_sum(cot_mine, cot_other, groups)
    far_rows, recv_rows, recv_columns = call(
        functools.partial(one_hot_kernel, tile, node_count, slots), "one_hots", 1,
        [
            shape(edge_total, halo_count), shape(edge_total, ROWS), shape(ROWS, edge_total),
        ],
        [edge_count, after(sender_rows, cot_mine), receiver_rows],
    )

    partial = call(
        functools.partial(fine_local_kernel, tile, step_edges), "fine_local", 5,
        [shape(edge_total, width)],
        [edges, sender_rows, recv_rows, nodes, after(fine_weights, incoming[1])],
        scratch=[
            room(node_count), room(node_count), pltpu.VMEM((2, step_edges, node_count), BF16)
        ],
        limit=24,
    )
    partial, cot_pair = lax.optimization_barrier((partial, cot_pair))
    cot_own = group_rest(cot_pair, 1.0, groups)
    per_edge = shape(edge_total, width)
    per_node = shape(node_count, width)
    halo_outs = [
        per_edge, per_edge, per_edge, shape(edge_total, 1, F32), per_node, per_node, per_node,
        shape(node_count, 1, F32), per_node, per_node, half, half, shape(halo_count, width),
    ]
    two_steps = pltpu.VMEM((2, step_edges, width), F32)
    (
        active, slope, unit, scale, node_active, node_slope, node_unit, node_scale, summed,
        refined, part_mine, part_other, halo_nodes,
    ) = call(
        functools.partial(fine_halo_kernel, tile, step_edges, places), "fine_halo", 6, halo_outs,
        [partial, far_rows, recv_columns, aggregate_rows, nodes, fine_weights, *incoming],
        scratch=[room(halo_count), two_steps, two_steps, room(group_rows)],
        limit=24,
    )
    part_mine, part_other, cot_own = lax.optimization_barrier((part_mine, part_other, cot_own))
    coarse_ins = [
        coarse_edges[0], coarse_senders.reshape(-1, 128), coarse_receivers.reshape(-1, 128),
        coarse_weights,
    ]
    coarse_ins, part_other = lax.optimization_barrier((coarse_ins, part_other))
    pair = pair_sum(part_mine, part_other, groups)
    coarse_pre = call(
        functools.partial(coarse_pre_kernel, groups), "coarse_pre", 2,
        [
            shape(coarse_total, width), shape(coarse_total, group_rows),
            shape(group_rows, coarse_total), shape(coarse_total, ROWS), shape(ROWS, coarse_total),
        ],
        [after(coarse_ins[0], pair), *coarse_ins[1:]],
    )
    send_columns = call(
        functools.partial(sender_kernel, node_count, slots), "sender_one_hots", 1,
        [shape(node_count + halo_count, edge_total)], [after(sender_rows, pair)],
        limit=8,
    )
    table_own = after(group_rest(pair, 0.125, groups), coarse_pre[0], send_columns)
    tables = [table_own, swap_core(table_own, groups)]
    cots = [cot_own, swap_core(cot_own, groups)]

    coarse_chunk = 4 * coarse_total // groups
    share = 7 * width // groups
    coarse_wide = shape(coarse_total, width)
    group_wide = shape(group_rows, width)
    coarse_rows = max(coarse_chunk, group_rows)
    table, coarse_table, table_grad, *coarse_kept = call(
        functools.partial(coarse_kernel, groups, coarse_chunk), "coarse_both_ways", 8,
        [group_wide] * 9 + [coarse_wide] * 3,
        [*tables, *cots, *coarse_pre, coarse_weights],
        scratch=[room(group_rows)] * 6
        + [room(coarse_total)] * 2
        + [room(coarse_total, 1, F32)]
        + [room(coarse_rows, width, F32)] * 2
        + [room(group_rows, width, F32)] * 2,
        limit=20,
    )
    node_partial, summed_grad, node_weights = call(
        node_back_kernel, "node_back", 5,
        [shape(node_count, width, F32), per_node, shape(3 * width, width)],
        [
            aggregate_rows, table_grad, cotangent, node_active, node_slope, node_unit, node_scale,
            summed, nodes, fine_weights,
        ],
        scratch=[room(node_count)] * 2 + [room(node_count, width, F32)] * 2,
    )
    half_weights = shape(7 * width // 2, width)
    hidden_grad, near, recv_total, weight_mine, weight_other, halo_near, halo_far = call(
        functools.partial(edge_back_kernel, tile, step_edges), "edge_back", 8,
        [per_edge, per_node, per_node, half_weights, half_weights]
        + [shape(halo_count // 2, width)] * 2,
        [
            edges, active, slope, unit, scale, send_columns, recv_rows, recv_columns,
            summed_grad, fine_weights, nodes, halo_nodes, node_weights,
        ],
        scratch=[room(edge_total), two_steps, two_steps, room(7 * width, width, F32)],
        limit=20,
    )

    more_grp = range(2, groups.bit_length() - 1)
    more_dom = range(2, domains.bit_length() - 1)
    received = flip(weight_other, "grp", 0)
    coarse_mine, coarse_other = call(
        functools.partial(coarse_products_kernel, groups), "coarse_products", 1,
        [shape(share // 2, width)] * 2,
        [after(coarse_edges[0], weight_other), table, *coarse_kept],
        scratch=[room(7 * width, width, F32)],
    )
    received = after(received, coarse_mine)
    mine, other = halved(add(weight_mine, received))

    received = flip(other, "grp", 1)
    fine_out = streamed(
        fine_out_kernel, "fine_out", 2, [per_node],
        [aggregate_rows, coarse_table, after(refined, other)],
    )
    coarse_received = flip(after(coarse_other, fine_out), "dom", 0)
    ties = [fine_out]
    mine, other = halved(add(mine, received))

    received = flip(other, "dom", 0)
    coarse_mine, coarse_other = halved(add(coarse_mine, coarse_received))
    coarse_received = flip(after(coarse_other, other), "dom", 1)
    ties.append(other)
    mine, other = halved(add(mine, received))

    received = flip(other, "dom", 1)
    ties.append(other)
    returned, places_back = exchange_slots(halo_near, halo_far, slots, ties)
    coarse_own = add(coarse_mine, coarse_received)
    for bit in more_dom:
        coarse_own = add(coarse_own, flip(after(coarse_own, other), "dom", bit))
    own = add(mine, received)
    for axis, bits in (("grp", more_grp), ("dom", more_dom)):
        for bit in bits:
            own = add(own, flip(own, axis, bit))
    for bit in (1, 0):
        coarse_own = jnp.concatenate([coarse_own, flip(coarse_own, "dom", bit)], axis=0)
    coarse_mine = jnp.concatenate(
        [coarse_own] + [turn_chip(coarse_own, groups, k) for k in range(1, chips)], axis=0
    )
    weight_shape = shape(7 * width, width, F32)
    coarse_total_grad = streamed(
        functools.partial(coarse_final_kernel, chips, (coarse_total * domains) ** (-0.5)),
        "coarse_weights", 2, [weight_shape], [coarse_mine, swap_core(coarse_mine, groups)],
    )
    node_grad = streamed(
        functools.partial(return_kernel, places_back), "halo_return", 3, [per_node],
        [halo_index, node_partial, near, recv_total, fine_weights, *returned],
        scratch=[room(halo_count)],
    )
    own = jnp.concatenate([own, flip(own, "dom", 1)], axis=0)
    own = jnp.concatenate([own, flip(own, "dom", 0)], axis=0)
    edge_grad = call(
        edge_out_kernel, "edge_out", 3, [per_edge], [after(hidden_grad, own), fine_weights],
        specs=(
            [by_tile(step_edges, width), whole(fine_weights)],
            [by_tile(step_edges, width)],
        ),
        grid=steps,
    )
    received = after(flip(own, "grp", 1), node_grad, edge_grad)
    own = jnp.concatenate([own, received], axis=0)
    fine_total_grad = streamed(
        functools.partial(fine_final_kernel, (edge_total * devices) ** (-0.5)),
        "fine_weights", 2, [weight_shape], [own, flip(own, "grp", 0)],
    )
    return (fine_out, node_grad, edge_grad, fine_total_grad, coarse_total_grad)


def solution(mesh):
    placed = (
        P(("dom", "grp"), None),
        P(("dom", "grp"), None),
        P(("dom", "grp")),
        P(("dom", "grp")),
        P(("dom", "grp")),
        P(("dom", "grp"), None, None),
        P(("dom", "grp")),
        P("dom", None, None),
        P("dom", None),
        P("dom", None),
        P(("dom", "grp"), None),
        P(),
        P(),
    )
    return jax.shard_map(
        body,
        mesh=mesh,
        in_specs=placed,
        out_specs=(
            P(("dom", "grp"), None),
            P(("dom", "grp"), None),
            P(("dom", "grp"), None),
            P(),
            P(),
        ),
        check_vma=False,
    )
```

```python
import functools

import jax
import jax.numpy as jnp
from jax import lax
from jax.experimental import pallas as pl
from jax.experimental.pallas import tpu as pltpu
from jax.sharding import PartitionSpec as P

F32 = jnp.float32
BF16 = jnp.bfloat16
ROWS = 128
MIB = 1024 * 1024
CHUNK = 64
I16 = jnp.int16


def mm(a, b):
    return lax.dot_general(a, b, (((1,), (0,)), ((), ())), preferred_element_type=F32)


def mm_nt(a, b):
    return lax.dot_general(a, b, (((1,), (1,)), ((), ())), preferred_element_type=F32)


def mm_tn(a, b):
    return lax.dot_general(a, b, (((0,), (0,)), ((), ())), preferred_element_type=F32)


def column(row):
    return jnp.broadcast_to(row, (128, row.shape[1])).T.astype(I16)


def flags(mask):
    return jnp.where(mask, jnp.ones((), BF16), jnp.zeros((), BF16))


def pick_rows(rows, width):
    lane = lax.broadcasted_iota(jnp.int32, (rows[0].shape[1], 128), 1).astype(I16)
    out = []
    for row in rows:
        index = column(row)
        out.append(
            jnp.concatenate([flags(index == lane + I16(128 * k)) for k in range(width // 128)], axis=1)
        )
    return out[0] if len(out) == 1 else jnp.concatenate(out, axis=0)


def pick_columns(rows, height):
    sub = lax.broadcasted_iota(jnp.int32, (height, rows[0].shape[1]), 0).astype(I16)
    out = []
    for row in rows:
        index = jnp.broadcast_to(row, (16, row.shape[1])).astype(I16)
        out.append(flags(sub == jnp.broadcast_to(index[0:1, :], sub.shape)))
    return out[0] if len(out) == 1 else jnp.concatenate(out, axis=1)


def gate(hidden):
    return 0.5 + 0.5 * jnp.tanh(0.5 * hidden)


def normalise(values):
    centre = values - jnp.mean(values, axis=-1, keepdims=True)
    spread = jnp.mean(centre * centre, axis=-1, keepdims=True)
    scale = lax.rsqrt(spread + 1e-05)
    return centre * scale, scale


def normalise_back(grad, unit, scale):
    along = jnp.mean(grad * unit, axis=-1, keepdims=True)
    return scale * (grad - jnp.mean(grad, axis=-1, keepdims=True) - unit * along)


def kernel_call(kernel, micros, limit, **kwargs):
    return pl.pallas_call(
        kernel,
        compiler_params=pltpu.CompilerParams(vmem_limit_bytes=limit * MIB),
        cost_estimate=pl.CostEstimate(
            flops=int(micros * 1.1e9), bytes_accessed=1 << 20, transcendentals=0
        ),
        **kwargs,
    )


def smem():
    return pl.BlockSpec(memory_space=pltpu.SMEM)


def whole(array):
    return pl.BlockSpec(array.shape, lambda t: (0,) * len(array.shape))


def by_tile(rows, columns):
    return pl.BlockSpec((rows, columns), lambda t: (t, 0))


def shape(rows, columns, dtype=BF16):
    return jax.ShapeDtypeStruct((rows, columns), dtype)


def chunks(total):
    return [slice(r, r + CHUNK) for r in range(0, total, CHUNK)]


def spans(start, size, tile):
    return [
        (
            slice(at, at + tile),
            slice(start + at, start + at + tile),
            slice((start + at) // tile * ROWS, ((start + at) // tile + 1) * ROWS),
        )
        for at in range(0, size, tile)
    ]


def at(start, here):
    return slice(start + here.start, start + here.stop)


def staggered(count, *stages):
    for t in range(count + len(stages) - 1):
        for k, stage in enumerate(stages):
            if 0 <= t - k < count:
                stage(t - k)


def my_core():
    return lax.rem(lax.axis_index("grp"), 2)


def split_halves(ref, mine_out, other_out):
    half = mine_out.shape[0]
    core = my_core()
    mine_out[...] = ref[pl.ds(core * half, half), :]
    other_out[...] = ref[pl.ds((1 - core) * half, half), :]


def one_hot_kernel(tile, node_count, slots, count, senders, receivers, far_out, rows_out, columns_out):
    lane = lax.broadcasted_iota(jnp.int32, (1, 128), 1)
    mask = lax.axis_index("dom") * slots
    for j in range(senders.shape[0]):
        here = slice(j * 128, (j + 1) * 128)
        row = jnp.bitwise_xor(senders[j : j + 1, :] - node_count, mask)
        far_out[here, :] = pick_rows([row], far_out.shape[1])
        row = receivers[j : j + 1, :] - j * 128 // tile * ROWS
        row = jnp.where(lane + j * 128 % tile < count[0], row, -1)
        rows_out[here, :] = pick_rows([row], ROWS)
        columns_out[:, here] = pick_columns([row], ROWS)


def sender_kernel(node_count, slots, senders, columns_out):
    mask = lax.axis_index("dom") * slots
    for j in range(senders.shape[0]):
        row = senders[j : j + 1, :]
        row = jnp.where(
            row < node_count, row, jnp.bitwise_xor(row - node_count, mask) + node_count
        )
        columns_out[:, j * 128 : (j + 1) * 128] = pick_columns([row], columns_out.shape[0])


def send_kernel(nodes, halo, near_out, far_out):
    doms, slots = halo.shape
    me = lax.axis_index("dom")
    for first, out in ((0, near_out), (doms // 2, far_out)):
        picks = [
            pick_rows([halo[pl.ds(jnp.bitwise_xor(me, first + r), 1), :]], nodes.shape[0])
            for r in range(doms // 2)
        ]
        out[...] = mm(jnp.concatenate(picks, axis=0), nodes[...]).astype(BF16)


def gather_slots(places, refs, out):
    slots = out.shape[0] // len(places)
    for r, (which, slot) in enumerate(places):
        out[r * slots : (r + 1) * slots, :] = refs[which][slot * slots : (slot + 1) * slots, :]


def group_sums(aggregates, values, mine_out, other_out, sums):
    rows = [aggregates[k : k + 1, :] for k in range(aggregates.shape[0])]
    sums[...] = mm(pick_columns(rows, sums.shape[0]), values).astype(BF16)
    split_halves(sums, mine_out, other_out)


def cotangent_kernel(aggregates, cotangent, mine_out, other_out, sums):
    group_sums(aggregates, cotangent[...], mine_out, other_out, sums)


def fine_local_kernel(
    tile, step_edges, edges, senders, recv_rows, nodes, weights,
    partial_out, send_proj, recv_proj, pick,
):
    width = nodes.shape[1]
    parts = step_edges // 128
    send_proj[...] = mm(nodes[...], weights[width : 2 * width, :]).astype(BF16)
    recv_proj[...] = mm(nodes[...], weights[2 * width : 3 * width, :]).astype(BF16)

    def choose(i):
        for j in range(parts):
            row = senders[i * parts + j : i * parts + j + 1, :]
            pick[i % 2, j * 128 : (j + 1) * 128, :] = pick_rows([row], nodes.shape[0])

    def multiply(i):
        for here, there, own in spans(i * step_edges, step_edges, tile):
            partial_out[there, :] = (
                mm(edges[there, :], weights[:width, :])
                + mm(recv_rows[there, :], recv_proj[own, :])
                + mm(pick[i % 2, here, :], send_proj[...])
            ).astype(BF16)

    staggered(edges.shape[0] // step_edges, choose, multiply)


def activate(hidden, active_out, slope_out, here):
    opened = gate(hidden)
    active = hidden * opened
    active_out[here, :] = active.astype(BF16)
    slope_out[here, :] = (opened + active * (1.0 - opened)).astype(BF16)


def fine_halo_kernel(
    tile, step_edges, places, partial, far_rows, recv_columns, aggregates, nodes, weights, *refs
):
    pieces = refs[: -(13 + 4)]
    (
        active_out, slope_out, unit_out, scale_out,
        node_active_out, node_slope_out, node_unit_out, node_scale_out, summed_out, refined_out,
        mine_out, other_out, halo,
        halo_proj, wide, wide_next, sums,
    ) = refs[-(13 + 4) :]
    node_count, width = nodes.shape
    gather_slots(places, pieces, halo)
    halo_proj[...] = mm(halo[...], weights[width : 2 * width, :]).astype(BF16)

    def first(i):
        start = i * step_edges
        wide[i % 2] = mm(far_rows[start : start + step_edges, :], halo_proj[...])
        for here in chunks(step_edges):
            there = at(start, here)
            activate(
                partial[there, :].astype(F32) + wide[i % 2, here, :], active_out, slope_out, there
            )

    def second(i):
        start = i * step_edges
        wide_next[i % 2] = mm(
            active_out[start : start + step_edges, :], weights[3 * width : 4 * width, :]
        )
        for here in chunks(step_edges):
            there = at(start, here)
            unit, scale = normalise(wide_next[i % 2, here, :])
            unit_out[there, :] = unit.astype(BF16)
            scale_out[there, :] = scale
        for here, there, own in spans(start, step_edges, tile):
            summed_out[own, :] = mm(recv_columns[:, there], unit_out[there, :]).astype(BF16)

    staggered(partial.shape[0] // step_edges, first, second)

    wide[0] = mm(nodes[...], weights[4 * width : 5 * width, :]) + mm(
        summed_out[...], weights[5 * width : 6 * width, :]
    )
    for here in chunks(node_count):
        activate(wide[0, here, :], node_active_out, node_slope_out, here)
    wide_next[0] = mm(node_active_out[...], weights[6 * width :, :])
    for here in chunks(node_count):
        unit, scale = normalise(wide_next[0, here, :])
        node_unit_out[here, :] = unit.astype(BF16)
        node_scale_out[here, :] = scale
        refined_out[here, :] = (nodes[here, :].astype(F32) + unit).astype(BF16)
    group_sums(aggregates, refined_out[...], mine_out, other_out, sums)


def coarse_pre_kernel(
    groups, edges, senders, receivers, weights,
    partial_out, send_rows_out, send_columns_out, recv_rows_out, recv_columns_out,
):
    total, width = edges.shape
    group_rows = send_columns_out.shape[0]
    tile = total // groups
    partial_out[...] = mm(edges[...], weights[:width, :]).astype(BF16)

    def run(i, carry):
        for j in range(tile // 128):
            at = i * (tile // 128) + j
            there = pl.ds(pl.multiple_of(at * 128, 128), 128)
            send, recv = senders[pl.ds(at, 1), :], receivers[pl.ds(at, 1), :]
            send_rows_out[there, :] = pick_rows([send], group_rows)
            recv_rows_out[there, :] = pick_rows([recv], ROWS)
            send_columns_out[:, there] = pick_columns([send], group_rows)
            recv_columns_out[:, there] = pick_columns([recv], ROWS)
        return carry

    lax.fori_loop(0, groups, run, 0)


def coarse_kernel(
    groups, chunk,
    table_mine, table_other, cot_mine, cot_other, partial, send_rows, send_columns, recv_rows,
    recv_columns, weights,
    table, output_out, grad_out, summed, node_active, node_pre, node_hidden_grad, send_total,
    recv_sum, active_all, hidden_grad_all, pre_all,
    cot, send_proj, recv_proj, summed_grad, node_slope, node_unit,
    slope_all, unit_all, scale_all, wide, wide_next, own_grad, send_sum,
):
    group_rows, width = table.shape
    half = group_rows // 2
    total = partial.shape[0]
    tile = total // groups
    spans = chunk // tile
    steps = total // chunk
    core = my_core()
    mine = pl.ds(core * half, half)
    other = pl.ds((1 - core) * half, half)
    table[mine, :] = table_mine[...]
    table[other, :] = table_other[...]
    cot[mine, :] = cot_mine[...]
    cot[other, :] = cot_other[...]
    send_proj[...] = mm(table[...], weights[width : 2 * width, :]).astype(BF16)
    recv_proj[...] = mm(table[...], weights[2 * width : 3 * width, :]).astype(BF16)

    def places(i):
        start = i * chunk
        return [
            (
                slice(s * tile, (s + 1) * tile),
                pl.ds(start + s * tile, tile),
                pl.ds((i * spans + s) * ROWS, ROWS),
            )
            for s in range(spans)
        ]

    for i in range(steps):
        start = i * chunk
        all_here = slice(start, start + chunk)
        for here, there, own in places(i):
            wide[here, :] = mm(send_rows[there, :], send_proj[...]) + mm(
                recv_rows[there, :], recv_proj[own, :]
            )
        for here in chunks(chunk):
            there = slice(start + here.start, start + here.stop)
            activate(
                wide[here, :] + partial[there, :].astype(F32), active_all, slope_all, there
            )
        wide_next[...] = mm(active_all[all_here, :], weights[3 * width : 4 * width, :])
        for here in chunks(chunk):
            there = slice(start + here.start, start + here.stop)
            unit, scale = normalise(wide_next[here, :])
            unit_all[there, :] = unit.astype(BF16)
            scale_all[there, :] = scale
        for here, there, own in places(i):
            summed[own, :] = mm(recv_columns[:, there], unit_all[there, :]).astype(BF16)

    nodes_here = slice(0, group_rows)
    wide[nodes_here, :] = mm(table[...], weights[4 * width : 5 * width, :]) + mm(
        summed[...], weights[5 * width : 6 * width, :]
    )
    for here in chunks(group_rows):
        activate(wide[here, :], node_active, node_slope, here)
    wide_next[nodes_here, :] = mm(node_active[...], weights[6 * width :, :])
    for here in chunks(group_rows):
        unit, scale = normalise(wide_next[here, :])
        output_out[here, :] = (table[here, :].astype(F32) + unit).astype(BF16)
        node_pre[here, :] = normalise_back(cot[here, :].astype(F32), unit, scale).astype(BF16)
    wide[nodes_here, :] = mm_nt(node_pre[...], weights[6 * width :, :])
    for here in chunks(group_rows):
        node_hidden_grad[here, :] = (wide[here, :] * node_slope[here, :].astype(F32)).astype(BF16)
    summed_grad[...] = mm_nt(
        node_hidden_grad[...], weights[5 * width : 6 * width, :]
    ).astype(BF16)
    own_grad[...] = mm_nt(node_hidden_grad[...], weights[4 * width : 5 * width, :])

    for i in range(steps):
        start = i * chunk
        all_here = slice(start, start + chunk)
        for here, there, own in places(i):
            wide[here, :] = mm(recv_rows[there, :], summed_grad[own, :])
        for here in chunks(chunk):
            there = slice(start + here.start, start + here.stop)
            pre_all[there, :] = normalise_back(
                wide[here, :], unit_all[there, :].astype(F32), scale_all[there, :]
            ).astype(BF16)
        wide_next[...] = mm_nt(pre_all[all_here, :], weights[3 * width : 4 * width, :])
        for here in chunks(chunk):
            there = slice(start + here.start, start + here.stop)
            hidden_grad_all[there, :] = (
                wide_next[here, :] * slope_all[there, :].astype(F32)
            ).astype(BF16)
        for here, there, own in places(i):
            recv_sum[own, :] = mm(recv_columns[:, there], hidden_grad_all[there, :]).astype(BF16)
        sent = mm(send_columns[:, all_here], hidden_grad_all[all_here, :])
        if i == 0:
            send_sum[...] = sent
        else:
            send_sum[...] += sent

    send_total[...] = send_sum[...].astype(BF16)
    grad_out[...] = (
        cot[...].astype(F32)
        + own_grad[...]
        + mm_nt(send_total[...], weights[width : 2 * width, :])
        + mm_nt(recv_sum[...], weights[2 * width : 3 * width, :])
    ).astype(BF16)


def coarse_products_kernel(
    groups, edges, table, summed, node_active, node_pre, node_hidden_grad, send_total, recv_total,
    active_all, hidden_grad_all, pre_all,
    weight_mine, weight_other,
    weight_all,
):
    width = table.shape[1]
    share = weight_mine.shape[0] * 2
    begin = (my_core() * (groups // 2) + lax.axis_index("grp") // 2) * share
    products = [
        (edges, hidden_grad_all),
        (table, send_total),
        (table, recv_total),
        (active_all, pre_all),
        (table, node_hidden_grad),
        (summed, node_hidden_grad),
        (node_active, node_pre),
    ]
    for b, (left, right) in enumerate(products):

        @pl.when((b * width < begin + share) & ((b + 1) * width > begin))
        def _():
            weight_all[b * width : (b + 1) * width, :] = mm_tn(left[...], right[...])

    chunk_rows = share // 4
    place = coarse_place()
    for r in range(4):
        first = pl.multiple_of(begin + jnp.bitwise_xor(place, r) * chunk_rows, 8)
        out = (weight_mine, weight_other)[r // 2]
        here = slice((r % 2) * chunk_rows, (r % 2 + 1) * chunk_rows)
        out[here, :] = weight_all[pl.ds(first, chunk_rows), :].astype(BF16)


def coarse_place():
    dom = lax.axis_index("dom")
    return lax.rem(dom, 2) * 2 + lax.rem(dom // 2, 2)


def fine_place():
    grp = lax.axis_index("grp")
    return lax.rem(grp, 2) * 8 + lax.rem(grp // 2, 2) * 4 + coarse_place()


def node_back_kernel(
    aggregates, table_grad, cotangent, node_active, node_slope, node_unit, node_scale, summed,
    nodes, weights,
    node_grad_out, summed_grad_out, weight_out,
    pre, hidden_grad, wide, wide_next,
):
    node_count, width = nodes.shape
    rows = [aggregates[k : k + 1, :] for k in range(aggregates.shape[0])]
    wide[...] = mm(pick_rows(rows, table_grad.shape[0]), table_grad[...])
    for here in chunks(node_count):
        grad = (cotangent[here, :].astype(F32) + 0.125 * wide[here, :]).astype(BF16)
        grad = grad.astype(F32)
        node_grad_out[here, :] = grad
        pre[here, :] = normalise_back(
            grad, node_unit[here, :].astype(F32), node_scale[here, :]
        ).astype(BF16)
    wide_next[...] = mm_nt(pre[...], weights[6 * width :, :])
    for here in chunks(node_count):
        hidden_grad[here, :] = (
            wide_next[here, :] * node_slope[here, :].astype(F32)
        ).astype(BF16)
    summed_grad_out[...] = mm_nt(
        hidden_grad[...], weights[5 * width : 6 * width, :]
    ).astype(BF16)
    node_grad_out[...] += mm_nt(hidden_grad[...], weights[4 * width : 5 * width, :])
    weight_out[:width, :] = mm_tn(nodes[...], hidden_grad[...]).astype(BF16)
    weight_out[width : 2 * width, :] = mm_tn(summed[...], hidden_grad[...]).astype(BF16)
    weight_out[2 * width :, :] = mm_tn(node_active[...], pre[...]).astype(BF16)


def edge_back_kernel(
    tile, step_edges, edges, active, slope, unit, scale, send_columns, recv_rows, recv_columns,
    summed_grad, weights, nodes, halo, node_weights,
    hidden_grad_out, near_out, recv_sum, weight_mine, weight_other, halo_near, halo_far,
    pre, wide, wide_next, weight_all,
):
    node_count, width = nodes.shape

    def first(i):
        start = i * step_edges
        for here, there, own in spans(start, step_edges, tile):
            wide[i % 2, here, :] = mm(recv_rows[there, :], summed_grad[own, :])
        for here in chunks(step_edges):
            there = at(start, here)
            pre[there, :] = normalise_back(
                wide[i % 2, here, :], unit[there, :].astype(F32), scale[there, :]
            ).astype(BF16)

    def second(i):
        start = i * step_edges
        wide_next[i % 2] = mm_nt(
            pre[start : start + step_edges, :], weights[3 * width : 4 * width, :]
        )
        for here in chunks(step_edges):
            there = at(start, here)
            hidden_grad_out[there, :] = (
                wide_next[i % 2, here, :] * slope[there, :].astype(F32)
            ).astype(BF16)

    staggered(edges.shape[0] // step_edges, first, second)

    hidden_grad = hidden_grad_out[...]
    near_out[...] = mm(send_columns[:node_count, :], hidden_grad).astype(BF16)
    far = mm(send_columns[node_count:, :], hidden_grad).astype(BF16)
    for here, there, own in spans(0, edges.shape[0], tile):
        recv_sum[own, :] = mm(recv_columns[:, there], hidden_grad_out[there, :]).astype(BF16)
    weight_all[3 * width : 4 * width, :] = mm_tn(active[...], pre[...])
    weight_all[:width, :] = mm_tn(edges[...], hidden_grad)
    weight_all[width : 2 * width, :] = mm_tn(nodes[...], near_out[...]) + mm_tn(halo[...], far)
    weight_all[2 * width : 3 * width, :] = mm_tn(nodes[...], recv_sum[...])
    weight_all[4 * width :, :] = node_weights[...].astype(F32)
    far_half = far.shape[0] // 2
    send_weights = weights[width : 2 * width, :]
    halo_near[...] = mm_nt(far[:far_half, :], send_weights).astype(BF16)
    halo_far[...] = mm_nt(far[far_half:, :], send_weights).astype(BF16)
    rows = weight_all.shape[0] // 16
    place = fine_place()
    for r in range(16):
        begin = pl.multiple_of(jnp.bitwise_xor(place, r) * rows, 16)
        out = (weight_mine, weight_other)[r // 8]
        out[(r % 8) * rows : (r % 8 + 1) * rows, :] = weight_all[pl.ds(begin, rows), :].astype(
            BF16
        )


def edge_out_kernel(hidden_grad, weights, edge_grad_out):
    edge_grad_out[...] = mm_nt(hidden_grad[...], weights[: hidden_grad.shape[1], :]).astype(BF16)


def fine_out_kernel(aggregates, table, refined, fine_out):
    rows = [aggregates[k : k + 1, :] for k in range(aggregates.shape[0])]
    lifted = mm(pick_rows(rows, table.shape[0]), table[...])
    fine_out[...] = (refined[...].astype(F32) + lifted).astype(BF16)


def return_kernel(places, halo, node_grad, near, recv_total, weights, *refs):
    doms = len(places)
    pieces, out, values = refs[:-2], refs[-2], refs[-1]
    width = out.shape[1]
    me = lax.axis_index("dom")
    gather_slots(places, pieces, values)
    row = jnp.concatenate(
        [halo[pl.ds(jnp.bitwise_xor(me, r), 1), :] for r in range(doms)], axis=1
    )
    parts = [row[:, 128 * k : 128 * (k + 1)] for k in range(row.shape[1] // 128)]
    out[...] = (
        node_grad[...]
        + mm(pick_columns(parts, out.shape[0]), values[...])
        + mm_nt(near[...], weights[width : 2 * width, :])
        + mm_nt(recv_total[...], weights[2 * width : 3 * width, :])
    ).astype(BF16)


def coarse_final_kernel(chips, scale, mine, other, out):
    share = mine.shape[0] // chips
    rows = share // 4
    core = my_core()
    chip = lax.axis_index("grp") // 2
    place = coarse_place()
    for k in range(chips):
        at = lax.rem(chip - k + chips, chips)
        for r in range(4):
            here = slice(k * share + r * rows, k * share + (r + 1) * rows)
            inside = jnp.bitwise_xor(place, r) * rows
            first = pl.multiple_of((core * chips + at) * share + inside, 8)
            second = pl.multiple_of(((1 - core) * chips + at) * share + inside, 8)
            out[pl.ds(first, rows), :] = mine[here, :].astype(F32) * scale
            out[pl.ds(second, rows), :] = other[here, :].astype(F32) * scale


def fine_final_kernel(scale, mine, other, out):
    rows = out.shape[0] // 16
    place = fine_place()
    for r in range(16):
        first = pl.multiple_of(jnp.bitwise_xor(place, r) * rows, 16)
        here = slice((r % 8) * rows, (r % 8 + 1) * rows)
        out[pl.ds(first, rows), :] = (mine, other)[r // 8][here, :].astype(F32) * scale


def swap_core(value, groups):
    return lax.ppermute(value, "grp", [(i, i ^ 1) for i in range(groups)])


def turn_chip(value, groups, places):
    return lax.ppermute(
        value, "grp", [(i, (i + 2 * places) % groups) for i in range(groups)]
    )


def group_rest(own, scale, groups):
    sent = own.astype(BF16)
    for k in range(1, groups // 2):
        own = own + turn_chip(sent, groups, k).astype(F32)
    return (own * scale).astype(BF16)


def pair_sum(mine, other, groups):
    return mine.astype(F32) + swap_core(other, groups).astype(F32)


def flip(value, axis, bit):
    size = lax.axis_size(axis)
    return lax.ppermute(value, axis, [(i, i ^ (1 << bit)) for i in range(size)])


def after(value, *others):
    return lax.optimization_barrier((value, *others))[0]


def add(a, b):
    return (a.astype(F32) + b.astype(F32)).astype(BF16)


def halved(values):
    half = values.shape[0] // 2
    return values[:half], values[half:]


def exchange_slots(near, far, slots, ties=()):
    doms = lax.axis_size("dom")
    arrays = [near]
    places = [(0, r) for r in range(doms // 2)] + [None] * (doms // 2)
    for bit in reversed(range(doms.bit_length() - 1)):
        moved_slots = [r for r in range(doms) if r >> bit & 1]
        if bit == doms.bit_length() - 2:
            sent = far
        else:
            sent = jnp.concatenate(
                [arrays[w][slot * slots : (slot + 1) * slots] for w, slot in
                 (places[r] for r in moved_slots)],
                axis=0,
            )
        stage = len(arrays) - 1
        if stage < len(ties):
            sent = after(sent, ties[stage])
        arrays.append(flip(sent, "dom", bit))
        for i, r in enumerate(moved_slots):
            places[r] = (len(arrays) - 1, i)
    return arrays, places


def body(
    nodes,
    edges,
    senders,
    receivers,
    edge_count,
    halo_rows,
    aggregates,
    coarse_edges,
    coarse_senders,
    coarse_receivers,
    cotangent,
    fine_weights,
    coarse_weights,
):
    node_count, width = nodes.shape
    edge_total = edges.shape[0]
    groups = lax.axis_size("grp")
    domains = lax.axis_size("dom")
    devices = groups * domains
    chips = groups // 2
    group_rows = ROWS * groups
    slots = halo_rows.shape[2]
    halo_count = domains * slots
    coarse_total = coarse_senders.shape[1]
    tiles = node_count // ROWS
    tile = edge_total // tiles
    step_edges = 2 * tile
    steps = tiles // 2

    halo_index = halo_rows[0]
    sender_rows = senders.reshape(-1, 128)
    receiver_rows = receivers.reshape(-1, 128)
    aggregate_rows = aggregates.reshape(-1, 128)
    half = shape(group_rows // 2, width)

    def call(kernel, name, micros, outs, ins, scratch=(), limit=20, specs=None, grid=None):
        outs = tuple(outs)
        in_specs, out_specs = specs or (
            [
                smem() if len(leaf.shape) == 1 else pl.BlockSpec(memory_space=pltpu.VMEM)
                for leaf in ins
            ],
            [pl.BlockSpec(memory_space=pltpu.VMEM) for leaf in outs],
        )
        result = kernel_call(
            kernel,
            micros,
            limit,
            out_shape=outs,
            in_specs=in_specs,
            out_specs=out_specs,
            scratch_shapes=list(scratch),
            name=name,
            **({} if grid is None else {"grid": (grid,)}),
        )(*ins)
        return result[0] if len(outs) == 1 else result

    def streamed(kernel, name, micros, outs, ins, scratch=(), limit=20):
        specs = ([whole(leaf) for leaf in ins], [whole(leaf) for leaf in outs])
        return call(kernel, name, micros, outs, ins, scratch, limit, specs, 1)

    def room(rows, columns=width, dtype=BF16):
        return pltpu.VMEM((rows, columns), dtype)

    send_near, send_far = streamed(
        send_kernel, "send_rows", 2,
        [shape(halo_count // 2, width), shape(halo_count // 2, width)], [nodes, halo_index],
    )
    send_far, later_cotangent = lax.optimization_barrier((send_far, cotangent))
    incoming, places = exchange_slots(send_near, send_far, slots)
    cot_mine, cot_other = call(
        cotangent_kernel, "cotangent_sums", 1, [half, half], [aggregate_rows, later_cotangent],
        scratch=[room(group_rows)],
    )
    cot_pair = pair_sum(cot_mine, cot_other, groups)
    far_rows, recv_rows, recv_columns = call(
        functools.partial(one_hot_kernel, tile, node_count, slots), "one_hots", 1,
        [
            shape(edge_total, halo_count), shape(edge_total, ROWS), shape(ROWS, edge_total),
        ],
        [edge_count, after(sender_rows, cot_mine), receiver_rows],
    )

    partial = call(
        functools.partial(fine_local_kernel, tile, step_edges), "fine_local", 5,
        [shape(edge_total, width)],
        [edges, sender_rows, recv_rows, nodes, after(fine_weights, incoming[1])],
        scratch=[
            room(node_count), room(node_count), pltpu.VMEM((2, step_edges, node_count), BF16)
        ],
        limit=24,
    )
    partial, cot_pair = lax.optimization_barrier((partial, cot_pair))
    cot_own = group_rest(cot_pair, 1.0, groups)
    per_edge = shape(edge_total, width)
    per_node = shape(node_count, width)
    halo_outs = [
        per_edge, per_edge, per_edge, shape(edge_total, 1, F32), per_node, per_node, per_node,
        shape(node_count, 1, F32), per_node, per_node, half, half, shape(halo_count, width),
    ]
    two_steps = pltpu.VMEM((2, step_edges, width), F32)
    (
        active, slope, unit, scale, node_active, node_slope, node_unit, node_scale, summed,
        refined, part_mine, part_other, halo_nodes,
    ) = call(
        functools.partial(fine_halo_kernel, tile, step_edges, places), "fine_halo", 6, halo_outs,
        [partial, far_rows, recv_columns, aggregate_rows, nodes, fine_weights, *incoming],
        scratch=[room(halo_count), two_steps, two_steps, room(group_rows)],
        limit=24,
    )
    part_mine, part_other, cot_own = lax.optimization_barrier((part_mine, part_other, cot_own))
    coarse_ins = [
        coarse_edges[0], coarse_senders.reshape(-1, 128), coarse_receivers.reshape(-1, 128),
        coarse_weights,
    ]
    coarse_ins, part_other = lax.optimization_barrier((coarse_ins, part_other))
    pair = pair_sum(part_mine, part_other, groups)
    coarse_pre = call(
        functools.partial(coarse_pre_kernel, groups), "coarse_pre", 2,
        [
            shape(coarse_total, width), shape(coarse_total, group_rows),
            shape(group_rows, coarse_total), shape(coarse_total, ROWS), shape(ROWS, coarse_total),
        ],
        [after(coarse_ins[0], pair), *coarse_ins[1:]],
    )
    send_columns = call(
        functools.partial(sender_kernel, node_count, slots), "sender_one_hots", 1,
        [shape(node_count + halo_count, edge_total)], [after(sender_rows, pair)],
        limit=8,
    )
    table_own = after(group_rest(pair, 0.125, groups), coarse_pre[0], send_columns)
    tables = [table_own, swap_core(table_own, groups)]
    cots = [cot_own, swap_core(cot_own, groups)]

    coarse_chunk = 4 * coarse_total // groups
    share = 7 * width // groups
    coarse_wide = shape(coarse_total, width)
    group_wide = shape(group_rows, width)
    coarse_rows = max(coarse_chunk, group_rows)
    table, coarse_table, table_grad, *coarse_kept = call(
        functools.partial(coarse_kernel, groups, coarse_chunk), "coarse_both_ways", 8,
        [group_wide] * 9 + [coarse_wide] * 3,
        [*tables, *cots, *coarse_pre, coarse_weights],
        scratch=[room(group_rows)] * 6
        + [room(coarse_total)] * 2
        + [room(coarse_total, 1, F32)]
        + [room(coarse_rows, width, F32)] * 2
        + [room(group_rows, width, F32)] * 2,
        limit=20,
    )
    node_partial, summed_grad, node_weights = call(
        node_back_kernel, "node_back", 5,
        [shape(node_count, width, F32), per_node, shape(3 * width, width)],
        [
            aggregate_rows, table_grad, cotangent, node_active, node_slope, node_unit, node_scale,
            summed, nodes, fine_weights,
        ],
        scratch=[room(node_count)] * 2 + [room(node_count, width, F32)] * 2,
    )
    half_weights = shape(7 * width // 2, width)
    hidden_grad, near, recv_total, weight_mine, weight_other, halo_near, halo_far = call(
        functools.partial(edge_back_kernel, tile, step_edges), "edge_back", 8,
        [per_edge, per_node, per_node, half_weights, half_weights]
        + [shape(halo_count // 2, width)] * 2,
        [
            edges, active, slope, unit, scale, send_columns, recv_rows, recv_columns,
            summed_grad, fine_weights, nodes, halo_nodes, node_weights,
        ],
        scratch=[room(edge_total), two_steps, two_steps, room(7 * width, width, F32)],
        limit=20,
    )

    more_grp = range(2, groups.bit_length() - 1)
    more_dom = range(2, domains.bit_length() - 1)
    received = flip(weight_other, "grp", 0)
    coarse_mine, coarse_other = call(
        functools.partial(coarse_products_kernel, groups), "coarse_products", 1,
        [shape(share // 2, width)] * 2,
        [after(coarse_edges[0], weight_other), table, *coarse_kept],
        scratch=[room(7 * width, width, F32)],
    )
    received = after(received, coarse_mine)
    mine, other = halved(add(weight_mine, received))

    received = flip(other, "grp", 1)
    fine_out = streamed(
        fine_out_kernel, "fine_out", 2, [per_node],
        [aggregate_rows, coarse_table, after(refined, other)],
    )
    coarse_received = flip(after(coarse_other, other), "dom", 0)
    ties = [other]
    received = after(received, fine_out)
    mine, other = halved(add(mine, received))

    received = flip(other, "dom", 0)
    coarse_mine, coarse_other = halved(add(coarse_mine, coarse_received))
    coarse_received = flip(after(coarse_other, other), "dom", 1)
    ties.append(other)
    mine, other = halved(add(mine, received))

    received = flip(other, "dom", 1)
    ties.append(other)
    returned, places_back = exchange_slots(halo_near, halo_far, slots, ties)
    coarse_own = add(coarse_mine, coarse_received)
    for bit in more_dom:
        coarse_own = add(coarse_own, flip(after(coarse_own, other), "dom", bit))
    own = add(mine, received)
    for axis, bits in (("grp", more_grp), ("dom", more_dom)):
        for bit in bits:
            own = add(own, flip(own, axis, bit))
    for bit in (1, 0):
        coarse_own = jnp.concatenate([coarse_own, flip(coarse_own, "dom", bit)], axis=0)
    coarse_mine = jnp.concatenate(
        [coarse_own] + [turn_chip(coarse_own, groups, k) for k in range(1, chips)], axis=0
    )
    weight_shape = shape(7 * width, width, F32)
    coarse_total_grad = streamed(
        functools.partial(coarse_final_kernel, chips, (coarse_total * domains) ** (-0.5)),
        "coarse_weights", 2, [weight_shape], [coarse_mine, swap_core(coarse_mine, groups)],
    )
    node_grad = streamed(
        functools.partial(return_kernel, places_back), "halo_return", 3, [per_node],
        [halo_index, node_partial, near, recv_total, fine_weights, *returned],
        scratch=[room(halo_count)],
    )
    own = jnp.concatenate([own, flip(own, "dom", 1)], axis=0)
    own = jnp.concatenate([own, flip(own, "dom", 0)], axis=0)
    edge_grad = call(
        edge_out_kernel, "edge_out", 3, [per_edge], [after(hidden_grad, own), fine_weights],
        specs=(
            [by_tile(step_edges, width), whole(fine_weights)],
            [by_tile(step_edges, width)],
        ),
        grid=steps,
    )
    received = after(flip(own, "grp", 1), node_grad, edge_grad)
    own = jnp.concatenate([own, received], axis=0)
    fine_total_grad = streamed(
        functools.partial(fine_final_kernel, (edge_total * devices) ** (-0.5)),
        "fine_weights", 2, [weight_shape], [own, flip(own, "grp", 0)],
    )
    return (fine_out, node_grad, edge_grad, fine_total_grad, coarse_total_grad)


def solution(mesh):
    placed = (
        P(("dom", "grp"), None),
        P(("dom", "grp"), None),
        P(("dom", "grp")),
        P(("dom", "grp")),
        P(("dom", "grp")),
        P(("dom", "grp"), None, None),
        P(("dom", "grp")),
        P("dom", None, None),
        P("dom", None),
        P("dom", None),
        P(("dom", "grp"), None),
        P(),
        P(),
    )
    return jax.shard_map(
        body,
        mesh=mesh,
        in_specs=placed,
        out_specs=(
            P(("dom", "grp"), None),
            P(("dom", "grp"), None),
            P(("dom", "grp"), None),
            P(),
            P(),
        ),
        check_vma=False,
    )
```
